32 devices in a mesh: ctx: 8 (over y, x, core), head: 4 (over z).
Axes of the slice: x: 2, y: 2, z: 4, core: 2. Of those that a mesh axis runs over, the one named last changes fastest.
Arguments:
- queries: bfloat16 [2048, 4096], P(('ctx', 'head')), may hold values from -4.6 to 4.6
- fresh_keys: bfloat16 [2048, 1024], P(('ctx', 'head')), may hold values from -4.6 to 4.6
- fresh_values: bfloat16 [2048, 1024], P(('ctx', 'head')), may hold values from -6 to 6
- cache_keys: bfloat16 [2048, 1024], P('ctx', 'head'), may hold values from -6 to 6
- cache_values: bfloat16 [2048, 1024], P('ctx', 'head'), may hold values from -6 to 6
- page_request: int32 [128], P('ctx'), may hold values from 0 to 2
- prompt_lengths: int32 [2], replicated, may hold values from 1 to 1792, 2048 in all
- output_weight: bfloat16 [4096, 4096], P('head'), may hold values from -0.375 to 0.375
Outputs:
- mixed: bfloat16 [2048, 4096], P(('ctx', 'head'))
The draws below stay inside these ranges and needn't reach their ends.
Inputs may be any that keep to these rules, and one draw needn't show every extreme that they name: `page_request`: value 2 marks a free page that no prompt reads.
All inputs are finite; a program needn't handle non-finite values.
Results may differ from the reference program's by a relative error of at most 0.015.
Values may be sent and summed in bfloat16 or wider, within the bound.
No kernel may reach another device: no remote copies, remote signals or barrier semaphores. Data moves between devices by JAX's collectives and lax.ppermute only.
A program may use at most 64 MiB of HBM per device.

```python
import math
import jax
import jax.numpy as jnp
import numpy as np
from jax import lax

D = 4096
QH = 32
KVH = 8
HD = 128
PAGE = 16
REQS = 2
BLK = 256
CPAGES = 16
NEW = 2048
CACHE = 2048
N_CTX = 8


def base_entries(key, columns):
    return jnp.clip(jax.random.normal(key, (NEW, columns), jnp.float32), -4.5, 4.5)


def draw_queries(key, part):
    entries = base_entries(jax.random.fold_in(key, 1), QH * HD)
    return entries.astype(jnp.bfloat16)


def draw_fresh_keys(key, part):
    entries = base_entries(jax.random.fold_in(key, 2), KVH * HD)
    return entries.astype(jnp.bfloat16)


def touch_ends(array, rng, smallest, high):
    shape = array.shape
    spot = [jax.random.randint(jax.random.fold_in(rng, axis), (), 0, shape[axis]) for axis in range(len(shape))]
    array = array.at[tuple(spot)].set(smallest)
    longest = shape.index(max(shape))
    spot[longest] = (spot[longest] + 1) % shape[longest]
    return array.at[tuple(spot)].set(high)


def shard_levels(own_key, extent, split, smallest, top_value):
    def one(dim, parts):
        draws = jax.random.uniform(jax.random.fold_in(jax.random.fold_in(own_key, 6), dim), (parts,), jnp.float32, smallest / len(split), top_value / len(split))
        return jnp.repeat(jnp.exp(draws), extent[dim] // parts).reshape((-1,) + (1,) * (len(extent) - dim - 1))

    gain = one(*split[0])
    for cut in split[1:]:
        gain = gain * one(*cut)
    return gain


def rank_bounds(number_of, slope):
    portions = [(1 << 20) // math.isqrt(rank ** slope) + 1 for rank in range(1, number_of + 1)]
    deviation = 1 + sum(portions) // (1 << 30)
    return np.cumsum(np.array([max(1, weight // deviation) for weight in portions]))


def skewed_ids(rng, shape, amount, skew):
    listing = rank_bounds(amount, skew)
    pick = jax.random.randint(jax.random.fold_in(rng, 1), shape, 0, int(listing[amount - 1]))
    grade = jnp.searchsorted(jnp.asarray(listing, jnp.int32), pick, side="right")
    return jax.random.permutation(jax.random.fold_in(rng, 2), amount)[grade].astype(jnp.int32)


def split_up(number_of, total, reach, slope):
    weights = [(1 << 20) // math.isqrt(rank ** slope) + 1 for rank in range(2, number_of + 1)]
    rest, counts = total - reach - (number_of - 1), [1] * (number_of - 1)
    while rest > 0:
        candidates = [i for i in range(number_of - 1) if counts[i] < reach]
        pool, budget = sum([weights[i] for i in candidates]), rest
        for i in candidates:
            extra = min(reach - counts[i], max(1, budget * weights[i] // pool), rest)
            counts[i] = counts[i] + extra
            rest = rest - extra
    return np.array([reach] + counts)


def uneven_parts(stream_key, count, total, limit, slope):
    if count == 2:
        one = jax.random.randint(stream_key, (), max(1, total - limit), min(limit, total - 1) + 1)
        return jnp.stack([one, total - one])
    lengths = jnp.asarray(split_up(count, total, limit, slope), jnp.int32)
    couples = (count - 1) // 2
    donor, taker = lengths[1:1 + 2 * couples:2], lengths[2:2 + 2 * couples:2]
    margin = jnp.minimum(donor - 1, limit - taker)
    moved = jax.random.randint(jax.random.fold_in(stream_key, 1), (couples,), 0, 1 << 20) % (margin + 1)
    lengths = lengths.at[1:1 + 2 * couples:2].set(donor - moved).at[2:2 + 2 * couples:2].set(taker + moved)
    return lengths[jax.random.permutation(jax.random.fold_in(stream_key, 2), count)]


def normal_values(rng, dims, width, limit, split=(), kind=jnp.bfloat16):
    loudness = shard_levels(rng, dims, split, -0.22, 0.18) if split else 1.0
    result = jax.random.normal(rng, dims, jnp.float32) * width * loudness
    return jnp.minimum(jnp.maximum(result, -limit), limit).astype(kind)


def setup_inputs(seed: int = 0) -> dict:
    seeds = jax.random.split(jax.random.key(seed), 9)
    return {
        "queries": draw_queries(jax.random.fold_in(seeds[8], 71), 0),
        "fresh_keys": draw_fresh_keys(jax.random.fold_in(seeds[8], 71), 0),
        "fresh_values": normal_values(seeds[2], (NEW, KVH * HD), 1.0, 6.0, ((0, 32),)),
        "cache_keys": normal_values(seeds[3], (CACHE, KVH * HD), 1.0, 6.0, ((0, 8), (1, 4))),
        "cache_values": normal_values(seeds[4], (CACHE, KVH * HD), 1.0, 6.0, ((0, 8), (1, 4))),
        "page_request": touch_ends(skewed_ids(seeds[5], (CPAGES * N_CTX,), REQS + 1, 2), jax.random.fold_in(seeds[5], 3), 0, REQS).astype(jnp.int32),
        "prompt_lengths": uneven_parts(seeds[6], REQS, NEW, NEW * 7 // 8, 2).astype(jnp.int32),
        "output_weight": normal_values(seeds[7], (QH * HD, D), (QH * HD // 16) ** -0.5, 0.375, ((0, 4),)),
    }


def positions_of_rows():
    row_ids = jnp.arange(NEW, dtype=jnp.int32)
    rank_ids = row_ids // BLK
    offsets = row_ids % BLK
    half_len = BLK // 2
    pieces = jnp.where(offsets < half_len, rank_ids, 2 * N_CTX - 1 - rank_ids)
    return (pieces * half_len + offsets % half_len).astype(jnp.int32)

def request_of(position, prompt_lengths):
    ends = jnp.cumsum(prompt_lengths).astype(jnp.int32)
    return lax.optimization_barrier(jnp.sum((position[:, None] >= ends[None, :]).astype(jnp.int32), axis=1)).astype(jnp.int32)

def reference(queries, fresh_keys, fresh_values, cache_keys, cache_values, page_request, prompt_lengths, output_weight):
    position = positions_of_rows()
    query_req = request_of(position, prompt_lengths)
    key_req = jnp.concatenate([jnp.repeat(page_request, PAGE).astype(jnp.int32), query_req])
    key_pos = jnp.concatenate([jnp.full((CACHE,), -1, jnp.int32), position])
    all_keys = jnp.concatenate([cache_keys, fresh_keys]).astype(jnp.float32).reshape(CACHE + NEW, KVH, HD)
    all_values = jnp.concatenate([cache_values, fresh_values]).astype(jnp.float32).reshape(CACHE + NEW, KVH, HD)
    group_size = QH // KVH
    score_scale = 1.0 / math.sqrt(HD)
    query_block = math.gcd(NEW, 256)

    def one_block(first_row):
        query_rows = lax.dynamic_slice_in_dim(queries, first_row, query_block, 0).astype(jnp.float32)
        query_rows = query_rows.reshape(query_block, KVH, group_size, HD)
        row_pos = lax.dynamic_slice_in_dim(position, first_row, query_block, 0)
        row_req = lax.dynamic_slice_in_dim(query_req, first_row, query_block, 0)
        visible = (row_req[:, None] == key_req[None, :]) & (key_pos[None, :] <= row_pos[:, None])

        def per_head(head_id):
            query_head = lax.dynamic_index_in_dim(query_rows, head_id, 1, keepdims=False)
            key_head = lax.dynamic_index_in_dim(all_keys, head_id, 1, keepdims=False)
            value_head = lax.dynamic_index_in_dim(all_values, head_id, 1, keepdims=False)
            scores = jnp.einsum('tgd,kd->tgk', query_head, key_head, precision=lax.Precision.HIGHEST) * score_scale
            masked = jnp.where(visible[:, None, :], scores, -1e+30)
            largest = lax.optimization_barrier(jnp.max(masked, axis=-1, keepdims=True))
            weights = jnp.where(visible[:, None, :], jnp.exp(masked - largest), 0.0)
            total_sum = lax.optimization_barrier(jnp.sum(weights, axis=-1))
            probs = lax.optimization_barrier(weights.astype(jnp.bfloat16)).astype(jnp.float32)
            summed = jnp.einsum('tgk,kd->tgd', probs, value_head, precision=lax.Precision.HIGHEST)
            return summed / total_sum[..., None]
        heads_out = lax.map(per_head, jnp.arange(KVH, dtype=jnp.int32))
        heads_out = jnp.transpose(heads_out, (1, 0, 2, 3)).reshape(query_block, QH * HD)
        return heads_out.astype(jnp.bfloat16)
    starts = jnp.arange(NEW // query_block, dtype=jnp.int32) * query_block
    attended = lax.map(one_block, starts).reshape(NEW, QH * HD)
    return jnp.dot(attended, output_weight, preferred_element_type=jnp.float32).astype(jnp.bfloat16)
```

```python
import functools
import math

import jax
import jax.numpy as jnp
from jax import lax
from jax.experimental import pallas as pl
from jax.experimental.pallas import tpu as pltpu
from jax.sharding import PartitionSpec as P

HD = 128
PAGE = 16
LANES = 128
HIDDEN = -1e30
BF16 = jnp.bfloat16
F32 = jnp.float32


def iota(shape, dim):
    return lax.broadcasted_iota(jnp.int32, shape, dim)


def pack_fresh_kernel(info, k_ref, v_ref, *outs):
    width = k_ref.shape[1] // len(outs)
    for x, out in enumerate(outs):
        columns = pl.ds(pl.multiple_of((info[1] ^ x) * width, width), width)
        out[:, :width] = k_ref[:, columns]
        out[:, width:] = v_ref[:, columns]


def pack_query_kernel(info, q_ref, *outs):
    width = q_ref.shape[1] // len(outs)
    for x, out in enumerate(outs):
        out[...] = q_ref[:, pl.ds(pl.multiple_of((info[1] ^ x) * width, width), width)]


def pack_cache_kernel(pages, k_ref, v_ref, out):
    tokens, width = k_ref.shape
    count = tokens // PAGE
    out[:tokens, :width] = k_ref[...]
    out[:tokens, width:] = v_ref[...]
    page = iota((count, 2 * width), 0)
    owner = jnp.zeros((count, 2 * width), jnp.int32)
    for p in range(count):
        owner = jnp.where(page == p, pages[p], owner)
    out[tokens:, :] = owner.astype(F32).astype(BF16)


def whole(shape):
    return pl.BlockSpec(shape, memory_space=pltpu.VMEM)


def smem():
    return pl.BlockSpec(memory_space=pltpu.SMEM)


def anywhere():
    return pl.BlockSpec(memory_space=pl.ANY)


def request_of(position, ends, requests):
    request = jnp.zeros(position.shape, jnp.int32)
    for r in range(requests):
        request += (position >= ends(r)).astype(jnp.int32)
    return request


def chunk_kernel(x_chunk, n_ctx, n_head, requests, info, q_hbm, *refs):
    cache_hbm, fresh_hbm = refs[:n_ctx], refs[n_ctx:2 * n_ctx]
    w_hbm, out, q_vm, cache, fresh, w_vm, scores, mixed, sems = refs[2 * n_ctx:]
    rows, q_width = q_vm.shape
    tokens, kv_width = fresh.shape[1:]
    groups = kv_width // (2 * HD)
    repeat = q_width // (groups * HD)
    pages = tokens // PAGE
    half = n_head * rows // 2
    c, h = info[0], info[1]
    ends = lambda r: info[2 + r]

    copies = [pltpu.make_async_copy(q_hbm, q_vm, sems.at[0])]
    for b in range(n_ctx):
        copies.append(pltpu.make_async_copy(cache_hbm[b], cache.at[b], sems.at[1 + b]))
    for b in range(n_ctx):
        copies.append(pltpu.make_async_copy(fresh_hbm[b], fresh.at[b], sems.at[1 + n_ctx + b]))
    copies.append(pltpu.make_async_copy(w_hbm, w_vm, sems.at[1 + 2 * n_ctx]))
    for copy in copies:
        copy.start()

    def start_of(rank, head):
        first = head * rows < half
        return jnp.where(first, rank, 2 * n_ctx - 1 - rank) * half + lax.rem(head * rows, half)

    p0 = start_of(c, h ^ x_chunk)
    lane = iota((rows, LANES), 1)
    row = iota((rows, LANES), 0)
    row_lane = lane - (LANES - rows)
    q_mask = (lane == request_of(p0 + row, ends, requests)) | (row_lane == row)
    q_mask = jnp.where(q_mask, 1.0, 0.0).astype(BF16)
    q_mask = jnp.concatenate([q_mask] * repeat, axis=0)

    def fresh_mask(b):
        parts = []
        for x in range(n_head):
            position = start_of(c ^ b, h ^ x) + row
            other = (lane < requests) & (request_of(position, ends, requests) != lane)
            later = (row_lane >= 0) & (position > p0 + row_lane)
            parts.append(jnp.where(other | later, HIDDEN, 0.0))
        return jnp.concatenate(parts, axis=0).astype(BF16)

    def cache_mask(b):
        owner = cache[b, tokens:, :LANES].astype(F32)
        page_lane = iota((pages, LANES), 1)
        other = (page_lane < requests) & (owner != page_lane.astype(F32))
        bias = jnp.where(other, HIDDEN, 0.0)
        bias = jnp.broadcast_to(bias[:, None, :], (pages, PAGE, LANES))
        return bias.reshape(tokens, LANES).astype(BF16)

    copies[0].wait()
    q_rows = []
    for g in range(groups):
        heads = [q_vm[:, (g * repeat + j) * HD:(g * repeat + j + 1) * HD] for j in range(repeat)]
        q_rows.append(jnp.concatenate([jnp.concatenate(heads, axis=0), q_mask], axis=1))

    scale = math.log2(math.e) / math.sqrt(HD)
    blocks = 2 * n_ctx
    largest = [None] * groups
    for b in range(blocks):
        copies[1 + b].wait()
        source = cache.at[b] if b < n_ctx else fresh.at[b - n_ctx]
        mask = cache_mask(b) if b < n_ctx else fresh_mask(b - n_ctx)
        for g in range(groups):
            keys = jnp.concatenate([source[:tokens, g * HD:(g + 1) * HD], mask], axis=1)
            s = lax.dot_general(q_rows[g], keys, (((1,), (1,)), ((), ())), preferred_element_type=F32)
            scores[g, :, b * tokens:(b + 1) * tokens] = s
            top = s[:, :LANES]
            for t in range(1, tokens // LANES):
                top = jnp.maximum(top, s[:, t * LANES:(t + 1) * LANES])
            largest[g] = top if b == 0 else jnp.maximum(largest[g], top)

    ones = jnp.ones((tokens, HD), BF16)
    for g in range(groups):
        top = jnp.max(largest[g], axis=1, keepdims=True) * scale
        summed = jnp.zeros((repeat * rows, 2 * HD), F32)
        for b in range(blocks):
            source = cache.at[b] if b < n_ctx else fresh.at[b - n_ctx]
            s = scores[g, :, b * tokens:(b + 1) * tokens]
            weights = jnp.exp2(s * scale - top).astype(BF16)
            values = jnp.concatenate([source[:tokens, (groups + g) * HD:(groups + g + 1) * HD], ones], axis=1)
            summed += jnp.dot(weights, values, preferred_element_type=F32)
        attended = (summed[:, :HD] / summed[:, HD:]).astype(BF16)
        for j in range(repeat):
            mixed[:, (g * repeat + j) * HD:(g * repeat + j + 1) * HD] = attended[j * rows:(j + 1) * rows]

    copies[-1].wait()
    step = min(1024, out.shape[1])
    for n in range(out.shape[1] // step):
        out[:, n * step:(n + 1) * step] = jnp.dot(
            mixed[...], w_vm[:, n * step:(n + 1) * step], preferred_element_type=F32
        ).astype(BF16)


def chunk(x, info, q, cache, fresh, weight, n_head, requests):
    n_ctx = len(cache)
    rows, q_width = q.shape
    tokens, kv_width = fresh[0].shape
    groups = kv_width // (2 * HD)
    repeat = q_width // (groups * HD)
    keys = 2 * n_ctx * tokens
    columns = weight.shape[1]
    return pl.pallas_call(
        functools.partial(chunk_kernel, x, n_ctx, n_head, requests),
        out_shape=jax.ShapeDtypeStruct((rows, columns), BF16),
        in_specs=[smem()] + [anywhere()] * (2 + 2 * n_ctx),
        out_specs=pl.BlockSpec(memory_space=pltpu.VMEM),
        scratch_shapes=[
            pltpu.VMEM((rows, q_width), BF16),
            pltpu.VMEM((n_ctx, cache[0].shape[0], kv_width), BF16),
            pltpu.VMEM((n_ctx, tokens, kv_width), BF16),
            pltpu.VMEM(weight.shape, BF16),
            pltpu.VMEM((groups, repeat * rows, keys), F32),
            pltpu.VMEM((rows, q_width), BF16),
            pltpu.SemaphoreType.DMA((2 + 2 * n_ctx,)),
        ],
        compiler_params=pltpu.CompilerParams(vmem_limit_bytes=40 * 1024 * 1024),
        cost_estimate=pl.CostEstimate(
            flops=8 * rows * q_width * keys + 2 * rows * q_width * columns,
            bytes_accessed=2 * (weight.size + keys * kv_width),
            transcendentals=rows * (q_width // HD) * keys,
        ),
    )(info, q, *cache, *fresh, weight)


def swap(value, axis, mask):
    return lax.ppermute(value, axis, [(i, i ^ mask) for i in range(lax.axis_size(axis))])


def gather_ctx(block):
    n_ctx = lax.axis_size("ctx")
    blocks = [None] * n_ctx
    for m in range(0, n_ctx, 2):
        blocks[m] = swap(block, "ctx", m) if m else block
    for m in range(0, n_ctx, 2):
        blocks[m + 1] = swap(blocks[m], "ctx", 1)
    return blocks


def shards(queries, fresh_keys, fresh_values, cache_keys, cache_values, page_request, prompt_lengths, output_weight):
    n_ctx, n_head = lax.axis_size("ctx"), lax.axis_size("head")
    requests = prompt_lengths.shape[0]
    rows = queries.shape[0]
    info = jnp.concatenate([
        jnp.stack([lax.axis_index("ctx"), lax.axis_index("head")]).astype(jnp.int32),
        jnp.stack([sum(prompt_lengths[i] for i in range(r + 1)) for r in range(requests)]),
    ])

    kv_width = 2 * fresh_keys.shape[1] // n_head
    fresh = pl.pallas_call(
        pack_fresh_kernel,
        out_shape=[jax.ShapeDtypeStruct((rows, kv_width), BF16)] * n_head,
        in_specs=[smem(), whole(fresh_keys.shape), whole(fresh_values.shape)],
        out_specs=[whole((rows, kv_width))] * n_head,
    )(info, fresh_keys, fresh_values)
    tokens = cache_keys.shape[0]
    cache = pl.pallas_call(
        pack_cache_kernel,
        out_shape=jax.ShapeDtypeStruct((tokens + tokens // PAGE, kv_width), BF16),
        in_specs=[smem(), whole(cache_keys.shape), whole(cache_values.shape)],
        out_specs=whole((tokens + tokens // PAGE, kv_width)),
    )(page_request, cache_keys, cache_values)
    q_width = queries.shape[1] // n_head
    query = pl.pallas_call(
        pack_query_kernel,
        out_shape=[jax.ShapeDtypeStruct((rows, q_width), BF16)] * n_head,
        in_specs=[smem(), whole(queries.shape)],
        out_specs=[whole((rows, q_width))] * n_head,
    )(info, queries)

    fresh = [swap(fresh[x], "head", x) if x else fresh[x] for x in range(n_head)]
    cache = gather_ctx(cache)
    fresh = gather_ctx(jnp.concatenate(fresh, axis=0))
    query = [swap(query[x], "head", x) if x else query[x] for x in range(n_head)]

    part = lambda x: chunk(x, info, query[x], cache, fresh, output_weight, n_head, requests)
    total = None
    for x in [*range(n_head - 1, 0, -1), 0]:
        partial = part(x)
        got = (swap(partial, "head", x) if x else partial).astype(F32)
        total = got if total is None else total + got
    return total.astype(BF16)


def solution(mesh):
    placed = (
        P(("ctx", "head"), None),
        P(("ctx", "head"), None),
        P(("ctx", "head"), None),
        P("ctx", "head"),
        P("ctx", "head"),
        P("ctx"),
        P(),
        P("head", None),
    )
    return jax.shard_map(
        shards, mesh=mesh, in_specs=placed, out_specs=P(("ctx", "head"), None), check_vma=False
    )
```

```python
import functools
import math

import jax
import jax.numpy as jnp
from jax import lax
from jax.experimental import pallas as pl
from jax.experimental.pallas import tpu as pltpu
from jax.sharding import PartitionSpec as P

HD = 128
PAGE = 16
LANES = 128
HIDDEN = -1e30
BF16 = jnp.bfloat16
F32 = jnp.float32


def iota(shape, dim):
    return lax.broadcasted_iota(jnp.int32, shape, dim)


def pack_kernel(pages, k_ref, v_ref, q_ref, ck_ref, cv_ref, *outs):
    n_head = (len(outs) - 1) // 2
    head = lax.axis_index("head")
    width = k_ref.shape[1] // n_head
    q_width = q_ref.shape[1] // n_head
    for x in range(n_head):
        other = head ^ x
        columns = pl.ds(pl.multiple_of(other * width, width), width)
        outs[x][:, :width] = k_ref[:, columns]
        outs[x][:, width:] = v_ref[:, columns]
        outs[n_head + x][...] = q_ref[:, pl.ds(pl.multiple_of(other * q_width, q_width), q_width)]
    out = outs[-1]
    tokens = ck_ref.shape[0]
    count = tokens // PAGE
    out[:tokens, :width] = ck_ref[...]
    out[:tokens, width:] = cv_ref[...]
    page = iota((count, 2 * width), 0)
    owner = jnp.zeros((count, 2 * width), jnp.int32)
    for p in range(count):
        owner = jnp.where(page == p, pages[p], owner)
    out[tokens:, :] = owner.astype(F32).astype(BF16)


def vmem():
    return pl.BlockSpec(memory_space=pltpu.VMEM)


def smem():
    return pl.BlockSpec(memory_space=pltpu.SMEM)


class Layout:
    def __init__(self, lengths, rows, q_width, kv_width, n_ctx, n_head):
        self.rows, self.n_ctx, self.n_head = rows, n_ctx, n_head
        self.groups = kv_width // (2 * HD)
        self.repeat = q_width // (self.groups * HD)
        self.half = n_head * rows // 2
        self.c, self.h = lax.axis_index("ctx"), lax.axis_index("head")
        self.ends, end = [], 0
        for r in range(lengths.shape[0]):
            end = end + lengths[r]
            self.ends.append(end)
        self.lane = iota((rows, LANES), 1)
        self.row = iota((rows, LANES), 0)
        self.row_lane = self.lane - (LANES - rows)

    def start_of(self, rank, head):
        first = head * self.rows < self.half
        piece = jnp.where(first, rank, 2 * self.n_ctx - 1 - rank)
        return piece * self.half + lax.rem(head * self.rows, self.half)

    def request(self, position):
        request = jnp.zeros(position.shape, jnp.int32)
        for end in self.ends:
            request += (position >= end).astype(jnp.int32)
        return request

    def query_rows(self, q, x):
        own = self.lane == self.request(self.start_of(self.c, self.h ^ x) + self.row)
        mask = jnp.where(own | (self.row_lane == self.row), 1.0, 0.0).astype(BF16)
        result = []
        for g in range(self.groups):
            heads = [
                jnp.concatenate([q[:, n * HD:(n + 1) * HD], mask], axis=1)
                for n in range(g * self.repeat, (g + 1) * self.repeat)
            ]
            result.append(jnp.concatenate(heads, axis=0))
        return result

    def fresh_mask(self, b, x_query):
        p0 = self.start_of(self.c, self.h ^ x_query)
        parts = []
        for x in range(self.n_head):
            position = self.start_of(self.c ^ b, self.h ^ x) + self.row
            other = (self.lane < len(self.ends)) & (self.request(position) != self.lane)
            later = (self.row_lane >= 0) & (position > p0 + self.row_lane)
            parts.append(jnp.where(other | later, HIDDEN, 0.0))
        return jnp.concatenate(parts, axis=0).astype(BF16)

    def cache_mask(self, owner):
        pages = owner.shape[0]
        lane = iota((pages, LANES), 1)
        other = (lane < len(self.ends)) & (owner.astype(F32) != lane.astype(F32))
        bias = jnp.where(other, HIDDEN, 0.0)
        bias = jnp.broadcast_to(bias[:, None, :], (pages, PAGE, LANES))
        return bias.reshape(pages * PAGE, LANES).astype(BF16)


def attend(q_rows, blocks, masks, scores, tokens, g, groups):
    scale = math.log2(math.e) / math.sqrt(HD)
    largest = None
    for b, (block, mask) in enumerate(zip(blocks, masks)):
        keys = jnp.concatenate([block[:tokens, g * HD:(g + 1) * HD], mask[...]], axis=1)
        s = lax.dot_general(q_rows, keys, (((1,), (1,)), ((), ())), preferred_element_type=F32)
        scores[:, b * tokens:(b + 1) * tokens] = s
        for t in range(tokens // LANES):
            part = s[:, t * LANES:(t + 1) * LANES]
            largest = part if largest is None else jnp.maximum(largest, part)
    top = jnp.max(largest, axis=1, keepdims=True) * scale
    ones = jnp.ones((tokens, HD), BF16)
    summed = jnp.zeros((q_rows.shape[0], 2 * HD), F32)
    for b, block in enumerate(blocks):
        weights = jnp.exp2(scores[:, b * tokens:(b + 1) * tokens] * scale - top).astype(BF16)
        values = jnp.concatenate([block[:tokens, (groups + g) * HD:(groups + g + 1) * HD], ones], axis=1)
        summed += jnp.dot(weights, values, preferred_element_type=F32)
    return summed, jnp.broadcast_to(top, (q_rows.shape[0], LANES))


def cache_kernel(n_ctx, n_head, lengths, *refs):
    query, cache = refs[:n_head], refs[n_head:n_head + n_ctx]
    summed, tops, scores, masks = refs[n_head + n_ctx:]
    rows, q_width = query[0].shape
    kv_width = cache[0].shape[1]
    tokens = masks.shape[1]
    at = Layout(lengths, rows, q_width, kv_width, n_ctx, n_head)
    for b in range(n_ctx):
        masks[b] = at.cache_mask(cache[b][tokens:, :LANES])
    for x in range(n_head):
        q_rows = at.query_rows(query[x], x)
        for g in range(at.groups):
            summed[x, g], tops[x, g] = attend(
                q_rows[g], cache, [masks.at[b] for b in range(n_ctx)], scores.at[g], tokens, g, at.groups
            )


def fresh_kernel(x, n_ctx, n_head, lengths, q, *refs):
    fresh = refs[:n_ctx]
    summed, tops, weight, out, scores, masks, mixed = refs[n_ctx:]
    rows, q_width = q.shape
    tokens, kv_width = fresh[0].shape
    at = Layout(lengths, rows, q_width, kv_width, n_ctx, n_head)
    for b in range(n_ctx):
        masks[b] = at.fresh_mask(b, x)
    q_rows = at.query_rows(q, x)
    for g in range(at.groups):
        sum_b, top_b = attend(
            q_rows[g], fresh, [masks.at[b] for b in range(n_ctx)], scores.at[g], tokens, g, at.groups
        )
        top_a = tops[x, g]
        top = jnp.maximum(top_a, top_b)
        factor_a, factor_b = jnp.exp2(top_a - top), jnp.exp2(top_b - top)
        value = summed[x, g, :, :HD] * factor_a + sum_b[:, :HD] * factor_b
        total = summed[x, g, :, HD:] * factor_a + sum_b[:, HD:] * factor_b
        attended = (value / total).astype(BF16)
        for j in range(at.repeat):
            n = g * at.repeat + j
            mixed[:, n * HD:(n + 1) * HD] = attended[j * rows:(j + 1) * rows]
    step = min(1024, out.shape[1])
    for n in range(out.shape[1] // step):
        columns = slice(n * step, (n + 1) * step)
        out[:, columns] = jnp.dot(mixed[...], weight[:, columns], preferred_element_type=F32).astype(BF16)


def limit(scratch):
    return pltpu.CompilerParams(vmem_limit_bytes=scratch + 24 * 1024 * 1024)


def attend_cache(lengths, query, cache, tokens):
    n_head, n_ctx = len(query), len(cache)
    rows, q_width = query[0].shape
    kv_width = cache[0].shape[1]
    groups = kv_width // (2 * HD)
    stacked = q_width // (groups * HD) * rows
    keys = n_ctx * tokens
    return pl.pallas_call(
        functools.partial(cache_kernel, n_ctx, n_head),
        out_shape=(
            jax.ShapeDtypeStruct((n_head, groups, stacked, 2 * HD), F32),
            jax.ShapeDtypeStruct((n_head, groups, stacked, LANES), F32),
        ),
        in_specs=[smem()] + [vmem()] * (n_head + n_ctx),
        out_specs=(vmem(), vmem()),
        scratch_shapes=[
            pltpu.VMEM((groups, stacked, keys), F32),
            pltpu.VMEM((n_ctx, tokens, LANES), BF16),
        ],
        compiler_params=limit(4 * groups * stacked * keys),
        cost_estimate=pl.CostEstimate(
            flops=16 * n_head * rows * q_width * keys,
            bytes_accessed=2 * keys * kv_width,
            transcendentals=n_head * rows * (q_width // HD) * keys,
        ),
    )(lengths, *query, *cache)


def attend_fresh(x, lengths, q, fresh, summed, tops, weight, n_head):
    n_ctx = len(fresh)
    rows, q_width = q.shape
    tokens, kv_width = fresh[0].shape
    groups = kv_width // (2 * HD)
    stacked = q_width // (groups * HD) * rows
    keys = n_ctx * tokens
    columns = weight.shape[1]
    return pl.pallas_call(
        functools.partial(fresh_kernel, x, n_ctx, n_head),
        out_shape=jax.ShapeDtypeStruct((rows, columns), BF16),
        in_specs=[smem()] + [vmem()] * (n_ctx + 4),
        out_specs=vmem(),
        scratch_shapes=[
            pltpu.VMEM((groups, stacked, keys), F32),
            pltpu.VMEM((n_ctx, tokens, LANES), BF16),
            pltpu.VMEM((rows, q_width), BF16),
        ],
        compiler_params=limit(4 * groups * stacked * keys),
        cost_estimate=pl.CostEstimate(
            flops=16 * rows * q_width * keys + 8 * rows * q_width * columns,
            bytes_accessed=2 * keys * kv_width,
            transcendentals=rows * (q_width // HD) * keys,
        ),
    )(lengths, q, *fresh, summed, tops, weight)


def swap(value, axis, mask):
    return lax.ppermute(value, axis, [(i, i ^ mask) for i in range(lax.axis_size(axis))])


def gather_ctx(block):
    n_ctx = lax.axis_size("ctx")
    blocks = [None] * n_ctx
    for m in range(0, n_ctx, 2):
        blocks[m] = swap(block, "ctx", m) if m else block
    for m in range(0, n_ctx, 2):
        blocks[m + 1] = swap(blocks[m], "ctx", 1)
    return blocks


def send(value, pairs):
    return lax.ppermute(value, "head", pairs)


def scatter_line(part, head):
    first = send(part(2), [(0, 1), (1, 3), (2, 0), (3, 2)])
    far = part(3)
    ends = send(far, [(0, 3), (3, 0)])
    near = send(part(1), [(0, 1), (1, 0), (2, 3), (3, 2)])
    inner = (head == 1) | (head == 2)
    joined = (far.astype(F32) + first.astype(F32)).astype(BF16)
    middle = send(joined, [(1, 2), (2, 1)])
    total = part(0).astype(F32) + near.astype(F32)
    return total + jnp.where(inner, middle.astype(F32), ends.astype(F32) + first.astype(F32))


def scatter_direct(part, n_head):
    total = None
    for x in [*range(n_head - 1, 0, -1), 0]:
        got = (swap(part(x), "head", x) if x else part(x)).astype(F32)
        total = got if total is None else total + got
    return total


def shards(queries, fresh_keys, fresh_values, cache_keys, cache_values, page_request, prompt_lengths, output_weight):
    n_head = lax.axis_size("head")
    rows = queries.shape[0]
    tokens = cache_keys.shape[0]
    kv_width = 2 * fresh_keys.shape[1] // n_head
    q_width = queries.shape[1] // n_head
    packed = pl.pallas_call(
        pack_kernel,
        out_shape=[jax.ShapeDtypeStruct((rows, kv_width), BF16)] * n_head
        + [jax.ShapeDtypeStruct((rows, q_width), BF16)] * n_head
        + [jax.ShapeDtypeStruct((tokens + tokens // PAGE, kv_width), BF16)],
        in_specs=[smem()] + [vmem()] * 5,
        out_specs=[vmem()] * (2 * n_head + 1),
    )(page_request, fresh_keys, fresh_values, queries, cache_keys, cache_values)
    fresh, query, cache = packed[:n_head], packed[n_head:2 * n_head], packed[-1]

    fresh = [swap(fresh[x], "head", x) if x else fresh[x] for x in range(n_head)]
    cache = gather_ctx(cache)
    query = [swap(query[x], "head", x) if x else query[x] for x in range(n_head)]
    fresh = gather_ctx(jnp.concatenate(fresh, axis=0))

    summed, tops = attend_cache(prompt_lengths, query, cache, tokens)
    part = lambda x: attend_fresh(x, prompt_lengths, query[x], fresh, summed, tops, output_weight, n_head)
    if n_head == 4:
        total = scatter_line(part, lax.axis_index("head"))
    else:
        total = scatter_direct(part, n_head)
    return total.astype(BF16)


def solution(mesh):
    placed = (
        P(("ctx", "head"), None),
        P(("ctx", "head"), None),
        P(("ctx", "head"), None),
        P("ctx", "head"),
        P("ctx", "head"),
        P("ctx"),
        P(),
        P("head", None),
    )
    return jax.shard_map(
        shards, mesh=mesh, in_specs=placed, out_specs=P(("ctx", "head"), None), check_vma=False
    )
```

```python
import functools
import math

import jax
import jax.numpy as jnp
from jax import lax
from jax.experimental import pallas as pl
from jax.experimental.pallas import tpu as pltpu
from jax.sharding import PartitionSpec as P

HD = 128
PAGE = 16
LANES = 128
HIDDEN = -1e30
MIB = 1024 * 1024
BF16 = jnp.bfloat16
F32 = jnp.float32


def iota(shape, dim):
    return lax.broadcasted_iota(jnp.int32, shape, dim)


def shaped(rows, columns, dtype=BF16):
    return jax.ShapeDtypeStruct((rows, columns), dtype)


def call(kernel, outs, ins, after=(), scratch=(), room=6 * MIB, cost=None):
    count = len(ins)

    def body(*refs):
        kernel(*refs[:count], *refs[count + len(after):])

    integers = lambda a: a.ndim == 1 and a.dtype == jnp.int32
    specs = [pl.BlockSpec(memory_space=pltpu.SMEM if integers(a) else pltpu.VMEM) for a in ins]
    return pl.pallas_call(
        body,
        out_shape=outs,
        in_specs=specs + [pl.BlockSpec(memory_space=pl.ANY)] * len(after),
        out_specs=[pl.BlockSpec(memory_space=pltpu.VMEM)] * len(outs),
        scratch_shapes=list(scratch),
        compiler_params=pltpu.CompilerParams(vmem_limit_bytes=room),
        cost_estimate=cost,
    )(*ins, *after)


def part_of(ref, index, count):
    width = ref.shape[1] // count
    return ref[:, pl.ds(pl.multiple_of(index * width, width), width)]


def pack_kernel(pages, k_ref, v_ref, ck_ref, cv_ref, *outs):
    *fresh, cache = outs
    head = lax.axis_index("head")
    tokens, width = ck_ref.shape
    for x, out in enumerate(fresh):
        out[:, :width] = part_of(k_ref, head ^ x, len(fresh))
        out[:, width:] = part_of(v_ref, head ^ x, len(fresh))
    cache[:tokens, :width] = ck_ref[...]
    cache[:tokens, width:] = cv_ref[...]
    count = pages.shape[0]
    page = iota((count, 2 * width), 0)
    owner = jnp.zeros((count, 2 * width), jnp.int32)
    for p in range(count):
        owner = jnp.where(page == p, pages[p], owner)
    cache[tokens:, :] = owner.astype(F32).astype(BF16)


def stage_kernel(lengths, q_ref, fresh_ref, cache_ref, fresh, cache, ends, *query):
    head = lax.axis_index("head")
    for x, out in enumerate(query):
        out[...] = part_of(q_ref, head ^ x, len(query))
    fresh[...] = fresh_ref[...]
    cache[...] = cache_ref[...]
    row = iota(ends.shape, 0)
    end, filled = 0, jnp.zeros(ends.shape, jnp.int32)
    for r in range(lengths.shape[0]):
        end = end + lengths[r]
        filled = jnp.where(row == r, end, filled)
    ends[...] = filled


def stack_kernel(*refs):
    out, rows = refs[-1], refs[0].shape[0]
    for i, ref in enumerate(refs[:-1]):
        out[i * rows:(i + 1) * rows, :] = ref[...]


class Layout:
    def __init__(self, ends, rows, q_width, kv_width, n_ctx, n_head):
        self.rows, self.n_ctx, self.n_head = rows, n_ctx, n_head
        self.groups = kv_width // (2 * HD)
        self.repeat = q_width // (self.groups * HD)
        self.half = n_head * rows // 2
        self.c, self.h = lax.axis_index("ctx"), lax.axis_index("head")
        self.ends = [ends[r:r + 1, :] for r in range(ends.shape[0])]
        self.lane = iota((rows, LANES), 1)
        self.row = iota((rows, LANES), 0)
        self.row_lane = self.lane - (LANES - rows)

    def start_of(self, rank, head):
        first = head * self.rows < self.half
        piece = jnp.where(first, rank, 2 * self.n_ctx - 1 - rank)
        return piece * self.half + lax.rem(head * self.rows, self.half)

    def step_of(self, b):
        if self.n_ctx != 8:
            return b
        near = jnp.where(lax.rem(self.c, 2) == 0, 2, 4)
        return [0, near, 6 - near, 6, 1, 7 - near, 1 + near, 7][b]

    def request(self, position):
        request = jnp.zeros(position.shape, jnp.int32)
        for end in self.ends:
            request += (position >= end).astype(jnp.int32)
        return request

    def query_rows(self, query, x):
        q = query[...]
        own = self.lane == self.request(self.start_of(self.c, self.h ^ x) + self.row)
        mask = jnp.where(own | (self.row_lane == self.row), 1.0, 0.0).astype(BF16)
        result = []
        for g in range(self.groups):
            heads = [
                jnp.concatenate([q[:, n * HD:(n + 1) * HD], mask], axis=1)
                for n in range(g * self.repeat, (g + 1) * self.repeat)
            ]
            result.append(jnp.concatenate(heads, axis=0))
        return result

    def fresh_mask(self, b, head):
        p0 = self.start_of(self.c, head)
        parts = []
        for x in range(self.n_head):
            position = self.start_of(self.c ^ self.step_of(b), self.h ^ x) + self.row
            other = (self.lane < len(self.ends)) & (self.request(position) != self.lane)
            later = (self.row_lane >= 0) & (position > p0 + self.row_lane)
            parts.append(jnp.where(other | later, HIDDEN, 0.0))
        return jnp.concatenate(parts, axis=0).astype(BF16)

    def cache_mask(self, owner):
        pages = owner.shape[0]
        lane = iota((pages, LANES), 1)
        other = (lane < len(self.ends)) & (owner.astype(F32) != lane.astype(F32))
        bias = jnp.where(other, HIDDEN, 0.0)
        bias = jnp.broadcast_to(bias[:, None, :], (pages, PAGE, LANES))
        return bias.reshape(pages * PAGE, LANES).astype(BF16)


def attend(q_rows, blocks, masks, scores, tokens, g, groups):
    scale = math.log2(math.e) / math.sqrt(HD)
    largest = None
    for b, (block, mask) in enumerate(zip(blocks, masks)):
        keys = jnp.concatenate([block[:tokens, g * HD:(g + 1) * HD], mask[...]], axis=1)
        s = lax.dot_general(q_rows, keys, (((1,), (1,)), ((), ())), preferred_element_type=F32)
        scores[:, b * tokens:(b + 1) * tokens] = s
        for t in range(tokens // LANES):
            part = s[:, t * LANES:(t + 1) * LANES]
            largest = part if largest is None else jnp.maximum(largest, part)
    top = jnp.max(largest, axis=1, keepdims=True) * scale
    ones = jnp.ones((tokens, HD), BF16)
    summed = jnp.zeros((q_rows.shape[0], 2 * HD), F32)
    for b, block in enumerate(blocks):
        weights = jnp.exp2(scores[:, b * tokens:(b + 1) * tokens] * scale - top).astype(BF16)
        values = jnp.concatenate([block[:tokens, (groups + g) * HD:(groups + g + 1) * HD], ones], axis=1)
        summed += jnp.dot(weights, values, preferred_element_type=F32)
    return summed, jnp.broadcast_to(top, (q_rows.shape[0], LANES))


def views(refs, tokens):
    return [ref.at[pl.ds(i, tokens)] for ref in refs for i in range(0, ref.shape[0], tokens)]


def cache_kernel(xs, count, n_ctx, n_head, q_width, ends, *refs):
    query, refs = refs[:len(xs)], refs[len(xs):]
    outs, (scores, masks) = refs[count:-2], refs[-2:]
    tokens = masks.shape[1]
    cache = views(refs[:count], tokens + tokens // PAGE)
    at = Layout(ends, query[0].shape[0], q_width, cache[0].shape[1], n_ctx, n_head)
    for b in range(n_ctx):
        masks[b] = at.cache_mask(cache[b][tokens:, :LANES])
    for i, x in enumerate(xs):
        summed, tops = outs[2 * i:2 * i + 2]
        q_rows = at.query_rows(query[i], x)
        for g in range(at.groups):
            summed[g], tops[g] = attend(
                q_rows[g], cache, [masks.at[b] for b in range(n_ctx)], scores.at[g], tokens, g, at.groups
            )


def fresh_kernel(xs, count, n_ctx, n_head, q_width, ends, *refs):
    query, refs = refs[:len(xs)], refs[len(xs):]
    fresh, state, refs = refs[:count], refs[count:count + 2 * len(xs)], refs[count + 2 * len(xs):]
    weight, outs, (scores, masks, mixed) = refs[0], refs[1:-3], refs[-3:]
    rows, tokens = query[0].shape[0], masks.shape[1]
    fresh = views(fresh, tokens)
    at = Layout(ends, rows, q_width, fresh[0].shape[1], n_ctx, n_head)
    for i, x in enumerate(xs):
        summed, tops = state[2 * i:2 * i + 2]
        for b in range(n_ctx):
            masks[b] = at.fresh_mask(b, at.h ^ x)
        q_rows = at.query_rows(query[i], x)
        for g in range(at.groups):
            sum_b, top_b = attend(
                q_rows[g], fresh, [masks.at[b] for b in range(n_ctx)], scores.at[g], tokens, g, at.groups
            )
            top = jnp.maximum(tops[g], top_b)
            factor_a, factor_b = jnp.exp2(tops[g] - top), jnp.exp2(top_b - top)
            value = summed[g, :, :HD] * factor_a + sum_b[:, :HD] * factor_b
            total = summed[g, :, HD:] * factor_a + sum_b[:, HD:] * factor_b
            attended = (value / total).astype(BF16)
            for j in range(at.repeat):
                n = g * at.repeat + j
                mixed[i * rows:(i + 1) * rows, n * HD:(n + 1) * HD] = attended[j * rows:(j + 1) * rows]
    width = outs[0].shape[1]
    step = min(1024, width)
    for n in range(width // step):
        columns = slice(n * step, (n + 1) * step)
        y = jnp.dot(mixed[...], weight[:, columns], preferred_element_type=F32).astype(BF16)
        for i, out in enumerate(outs):
            out[:, columns] = y[i * rows:(i + 1) * rows]


def add_kernel(count, *refs):
    out, rest = refs[-1], refs[count:-1]
    total = refs[0][...].astype(F32)
    for ref in refs[1:count]:
        total += ref[...].astype(F32)
    out[...] = total.astype(BF16)
    for ref in rest:
        head = lax.axis_index("head")

        @pl.when((head == 0) | (head == lax.axis_size("head") - 1))
        def _():
            out[...] = (total + ref[...].astype(F32)).astype(BF16)


def add(parts, at_ends=()):
    return call(functools.partial(add_kernel, len(parts)), [shaped(*parts[0].shape)], [*parts, *at_ends])[0]


def swap(value, axis, mask):
    return lax.ppermute(value, axis, [(i, i ^ mask) for i in range(lax.axis_size(axis))])


def gather(block, join):
    n_ctx = lax.axis_size("ctx")
    if n_ctx != 8:
        blocks = [block if m == 0 else swap(block, "ctx", m) for m in range(0, n_ctx, 2)]
        return [b for pair in blocks for b in (pair, swap(pair, "ctx", 1))]
    pair = join(lax.ppermute(block, "ctx", [(i, i ^ (4 if i % 2 else 2)) for i in range(8)]))
    far = lax.ppermute(pair, "ctx", [(i, i ^ (2 if i % 2 else 4)) for i in range(8)])
    return [pair, far, swap(pair, "ctx", 1), swap(far, "ctx", 1)]


def send(value, pairs):
    return lax.ppermute(value, "head", pairs)


def scatter_line(part):
    first = send(part((2,))[0], [(0, 1), (1, 3), (2, 0), (3, 2)])
    far, = part((3,))
    ends = send(far, [(0, 3), (3, 0)])
    near, own = part((1, 0), far)
    near = send(near, [(0, 1), (1, 0), (2, 3), (3, 2)])
    middle = send(add([far, first]), [(1, 2), (2, 1)])
    return add([own, near, ends, middle], [first])


def scatter_direct(part, n_head):
    parts = []
    for x in [*range(n_head - 1, 0, -1), 0]:
        got, = part((x,))
        parts.append(swap(got, "head", x) if x else got)
    return add(parts)


def shards(queries, fresh_keys, fresh_values, cache_keys, cache_values, page_request, prompt_lengths, output_weight):
    n_ctx, n_head = lax.axis_size("ctx"), lax.axis_size("head")
    rows, columns = queries.shape[0], output_weight.shape[1]
    tokens, pages = cache_keys.shape[0], page_request.shape[0]
    kv_width = 2 * fresh_keys.shape[1] // n_head
    q_width = queries.shape[1] // n_head
    groups = kv_width // (2 * HD)
    stacked = q_width // (groups * HD) * rows
    keys = n_ctx * tokens

    *packed, sent = call(
        pack_kernel, [shaped(rows, kv_width)] * n_head + [shaped(tokens + pages, kv_width)],
        [page_request, fresh_keys, fresh_values, cache_keys, cache_values], room=58 * MIB,
    )
    fresh, cache, ends, *query = call(
        stage_kernel,
        [shaped(rows, kv_width), shaped(tokens + pages, kv_width), shaped(prompt_lengths.shape[0], LANES, jnp.int32)]
        + [shaped(rows, q_width)] * n_head,
        [prompt_lengths, queries, packed[0], sent],
    )

    def stack(parts, *after):
        rows, columns = parts[0].shape
        return call(stack_kernel, [shaped(len(parts) * rows, columns)], parts, after=after)[0]

    fresh = stack([fresh, *(swap(packed[x], "head", x) for x in range(1, n_head))])
    cache = gather(sent, lambda got: stack([cache, got], fresh))
    for x in range(1, n_head):
        query[x] = swap(stack([query[x]], fresh) if x > 1 else query[x], "head", x)
    fresh = gather(fresh, lambda got: stack([fresh, got], *query[1:3]))

    scratch = [pltpu.VMEM((groups, stacked, keys), F32), pltpu.VMEM((n_ctx, tokens, LANES), BF16)]
    room = 4 * groups * stacked * keys + 6 * MIB
    xs = range(n_head)
    state = call(
        functools.partial(cache_kernel, xs, len(cache), n_ctx, n_head, q_width),
        [jax.ShapeDtypeStruct((groups, stacked, lanes), F32) for _ in xs for lanes in (2 * HD, LANES)],
        [ends, *query, *cache], scratch=scratch, room=room,
        cost=pl.CostEstimate(
            flops=16 * n_head * rows * q_width * keys,
            bytes_accessed=2 * keys * kv_width,
            transcendentals=n_head * rows * (q_width // HD) * keys,
        ),
    )

    def part(xs, *after):
        return call(
            functools.partial(fresh_kernel, xs, len(fresh), n_ctx, n_head, q_width), [shaped(rows, columns)] * len(xs),
            [ends, *(query[x] for x in xs), *fresh, *(a for x in xs for a in state[2 * x:2 * x + 2]), output_weight],
            after=after, scratch=[*scratch, pltpu.VMEM((len(xs) * rows, q_width), BF16)], room=room,
            cost=pl.CostEstimate(
                flops=len(xs) * (16 * rows * q_width * keys + 8 * rows * q_width * columns),
                bytes_accessed=2 * keys * kv_width,
                transcendentals=len(xs) * rows * (q_width // HD) * keys,
            ),
        )

    return scatter_line(part) if n_head == 4 else scatter_direct(part, n_head)


def solution(mesh):
    placed = (
        P(("ctx", "head"), None),
        P(("ctx", "head"), None),
        P(("ctx", "head"), None),
        P("ctx", "head"),
        P("ctx", "head"),
        P("ctx"),
        P(),
        P("head", None),
    )
    return jax.shard_map(
        shards, mesh=mesh, in_specs=placed, out_specs=P(("ctx", "head"), None), check_vma=False
    )
```

```python
import functools
import math

import jax
import jax.numpy as jnp
from jax import lax
from jax.experimental import pallas as pl
from jax.experimental.pallas import tpu as pltpu
from jax.sharding import PartitionSpec as P

HD = 128
PAGE = 16
LANES = 128
HIDDEN = -1e30
MIB = 1024 * 1024
BF16 = jnp.bfloat16
F32 = jnp.float32


def iota(shape, dim):
    return lax.broadcasted_iota(jnp.int32, shape, dim)


def shaped(rows, columns, dtype=BF16):
    return jax.ShapeDtypeStruct((rows, columns), dtype)


def call(kernel, outs, ins, after=(), scratch=(), room=6 * MIB, cost=None):
    count = len(ins)

    def body(*refs):
        kernel(*refs[:count], *refs[count + len(after):])

    integers = lambda a: a.ndim == 1 and a.dtype == jnp.int32
    specs = [pl.BlockSpec(memory_space=pltpu.SMEM if integers(a) else pltpu.VMEM) for a in ins]
    return pl.pallas_call(
        body,
        out_shape=outs,
        in_specs=specs + [pl.BlockSpec(memory_space=pl.ANY)] * len(after),
        out_specs=[pl.BlockSpec(memory_space=pltpu.VMEM)] * len(outs),
        scratch_shapes=list(scratch),
        compiler_params=pltpu.CompilerParams(vmem_limit_bytes=room),
        cost_estimate=cost,
    )(*ins, *after)


def part_of(ref, index, count):
    width = ref.shape[1] // count
    return ref[:, pl.ds(pl.multiple_of(index * width, width), width)]


def pack_kernel(pages, k_ref, v_ref, ck_ref, cv_ref, *outs):
    *fresh, cache = outs
    head = lax.axis_index("head")
    tokens, width = ck_ref.shape
    for x, out in enumerate(fresh):
        out[:, :width] = part_of(k_ref, head ^ x, len(fresh))
        out[:, width:] = part_of(v_ref, head ^ x, len(fresh))
    cache[:tokens, :width] = ck_ref[...]
    cache[:tokens, width:] = cv_ref[...]
    count = pages.shape[0]
    page = iota((count, 2 * width), 0)
    owner = jnp.zeros((count, 2 * width), jnp.int32)
    for p in range(count):
        owner = jnp.where(page == p, pages[p], owner)
    cache[tokens:, :] = owner.astype(F32).astype(BF16)


def stage_kernel(lengths, q_ref, fresh_ref, cache_ref, fresh, cache, ends, *query):
    head = lax.axis_index("head")
    for x, out in enumerate(query):
        out[...] = part_of(q_ref, head ^ x, len(query))
    fresh[...] = fresh_ref[...]
    cache[...] = cache_ref[...]
    row = iota(ends.shape, 0)
    end, filled = 0, jnp.zeros(ends.shape, jnp.int32)
    for r in range(lengths.shape[0]):
        end = end + lengths[r]
        filled = jnp.where(row == r, end, filled)
    ends[...] = filled


def stack_kernel(*refs):
    out, rows = refs[-1], refs[0].shape[0]
    for i, ref in enumerate(refs[:-1]):
        out[i * rows:(i + 1) * rows, :] = ref[...]


def stack(parts, *after):
    rows, columns = parts[0].shape
    return call(stack_kernel, [shaped(len(parts) * rows, columns)], parts, after=after)[0]


class Layout:
    def __init__(self, ends, rows, q_width, kv_width, n_ctx, n_head):
        self.rows, self.n_ctx, self.n_head = rows, n_ctx, n_head
        self.groups = kv_width // (2 * HD)
        self.repeat = q_width // (self.groups * HD)
        self.half = n_head * rows // 2
        self.c, self.h = lax.axis_index("ctx"), lax.axis_index("head")
        self.ends = [ends[r:r + 1, :] for r in range(ends.shape[0])]
        self.lane = iota((rows, LANES), 1)
        self.row = iota((rows, LANES), 0)
        self.row_lane = self.lane - (LANES - rows)

    def start_of(self, rank, head):
        first = head * self.rows < self.half
        piece = jnp.where(first, rank, 2 * self.n_ctx - 1 - rank)
        return piece * self.half + lax.rem(head * self.rows, self.half)

    def step_of(self, b):
        if self.n_ctx != 8 or self.n_head != 4:
            return b
        near = jnp.where(lax.rem(self.c, 2) == 0, 2, 4)
        return [0, near, 1, 7 - near, 6 - near, 6, 1 + near, 7][b]

    def request(self, position):
        request = jnp.zeros(position.shape, jnp.int32)
        for end in self.ends:
            request += (position >= end).astype(jnp.int32)
        return request

    def query_rows(self, query, x):
        q = query[...]
        own = self.lane == self.request(self.start_of(self.c, self.h ^ x) + self.row)
        mask = jnp.where(own | (self.row_lane == self.row), 1.0, 0.0).astype(BF16)
        result = []
        for g in range(self.groups):
            heads = [
                jnp.concatenate([q[:, n * HD:(n + 1) * HD], mask], axis=1)
                for n in range(g * self.repeat, (g + 1) * self.repeat)
            ]
            result.append(jnp.concatenate(heads, axis=0))
        return result

    def fresh_mask(self, b, head):
        p0 = self.start_of(self.c, head)
        parts = []
        for x in range(self.n_head):
            position = self.start_of(self.c ^ self.step_of(b), self.h ^ x) + self.row
            other = (self.lane < len(self.ends)) & (self.request(position) != self.lane)
            later = (self.row_lane >= 0) & (position > p0 + self.row_lane)
            parts.append(jnp.where(other | later, HIDDEN, 0.0))
        return jnp.concatenate(parts, axis=0).astype(BF16)

    def cache_mask(self, owner):
        pages = owner.shape[0]
        lane = iota((pages, LANES), 1)
        other = (lane < len(self.ends)) & (owner.astype(F32) != lane.astype(F32))
        bias = jnp.where(other, HIDDEN, 0.0)
        bias = jnp.broadcast_to(bias[:, None, :], (pages, PAGE, LANES))
        return bias.reshape(pages * PAGE, LANES).astype(BF16)


def attend(q_rows, blocks, masks, scores, tokens, g, groups):
    scale = math.log2(math.e) / math.sqrt(HD)
    largest = None
    for b, (block, mask) in enumerate(zip(blocks, masks)):
        keys = jnp.concatenate([block[:tokens, g * HD:(g + 1) * HD], mask[...]], axis=1)
        s = lax.dot_general(q_rows, keys, (((1,), (1,)), ((), ())), preferred_element_type=F32)
        scores[:, b * tokens:(b + 1) * tokens] = s
        for t in range(tokens // LANES):
            part = s[:, t * LANES:(t + 1) * LANES]
            largest = part if largest is None else jnp.maximum(largest, part)
    top = jnp.max(largest, axis=1, keepdims=True) * scale
    ones = jnp.ones((tokens, HD), BF16)
    summed = jnp.zeros((q_rows.shape[0], 2 * HD), F32)
    for b, block in enumerate(blocks):
        weights = jnp.exp2(scores[:, b * tokens:(b + 1) * tokens] * scale - top).astype(BF16)
        values = jnp.concatenate([block[:tokens, (groups + g) * HD:(groups + g + 1) * HD], ones], axis=1)
        summed += jnp.dot(weights, values, preferred_element_type=F32)
    return summed, jnp.broadcast_to(top, (q_rows.shape[0], LANES))


def views(refs, tokens):
    return [ref.at[pl.ds(i, tokens)] for ref in refs for i in range(0, ref.shape[0], tokens)]


def first_kernel(xs, cached, count, n_ctx, n_head, q_width, ends, *refs):
    query, refs = refs[:len(xs)], refs[len(xs):]
    outs, (scores, masks) = refs[count:-2], refs[-2:]
    tokens = masks.shape[1]
    cache = views(refs[:cached], tokens + tokens // PAGE)
    fresh = views(refs[cached:count], tokens)
    at = Layout(ends, query[0].shape[0], q_width, cache[0].shape[1], n_ctx, n_head)
    for b in range(n_ctx):
        masks[b] = at.cache_mask(cache[b][tokens:, :LANES])
    for i, x in enumerate(xs):
        summed, tops = outs[2 * i:2 * i + 2]
        for b in range(len(fresh)):
            masks[n_ctx + b] = at.fresh_mask(b, at.h ^ x)
        q_rows = at.query_rows(query[i], x)
        for g in range(at.groups):
            summed[g], tops[g] = attend(
                q_rows[g], cache + fresh, [masks.at[b] for b in range(n_ctx + len(fresh))], scores.at[g], tokens, g, at.groups
            )


def last_kernel(xs, count, n_ctx, n_head, q_width, ends, *refs):
    query, refs = refs[:len(xs)], refs[len(xs):]
    fresh, state, refs = refs[:count], refs[count:count + 2 * len(xs)], refs[count + 2 * len(xs):]
    weight, outs, (scores, masks, mixed) = refs[0], refs[1:-3], refs[-3:]
    rows, tokens = query[0].shape[0], masks.shape[1]
    fresh = views(fresh, tokens)
    at = Layout(ends, rows, q_width, fresh[0].shape[1], n_ctx, n_head)
    for i, x in enumerate(xs):
        summed, tops = state[2 * i:2 * i + 2]
        for b in range(len(fresh)):
            masks[b] = at.fresh_mask(n_ctx - len(fresh) + b, at.h ^ x)
        q_rows = at.query_rows(query[i], x)
        for g in range(at.groups):
            sum_b, top_b = attend(
                q_rows[g], fresh, [masks.at[b] for b in range(len(fresh))], scores.at[g], tokens, g, at.groups
            )
            top = jnp.maximum(tops[g], top_b)
            factor_a, factor_b = jnp.exp2(tops[g] - top), jnp.exp2(top_b - top)
            value = summed[g, :, :HD] * factor_a + sum_b[:, :HD] * factor_b
            total = summed[g, :, HD:] * factor_a + sum_b[:, HD:] * factor_b
            attended = (value / total).astype(BF16)
            for j in range(at.repeat):
                n = g * at.repeat + j
                mixed[i * rows:(i + 1) * rows, n * HD:(n + 1) * HD] = attended[j * rows:(j + 1) * rows]
    width = outs[0].shape[1]
    step = min(1024, width)
    for n in range(width // step):
        columns = slice(n * step, (n + 1) * step)
        y = jnp.dot(mixed[...], weight[:, columns], preferred_element_type=F32).astype(BF16)
        for i, out in enumerate(outs):
            out[:, columns] = y[i * rows:(i + 1) * rows]


def add_kernel(count, *refs):
    out, rest = refs[-1], refs[count:-1]
    total = refs[0][...].astype(F32)
    for ref in refs[1:count]:
        total += ref[...].astype(F32)
    out[...] = total.astype(BF16)
    for ref in rest:
        head = lax.axis_index("head")

        @pl.when((head == 0) | (head == lax.axis_size("head") - 1))
        def _():
            out[...] = (total + ref[...].astype(F32)).astype(BF16)


def add(parts, at_ends=()):
    return call(functools.partial(add_kernel, len(parts)), [shaped(*parts[0].shape)], [*parts, *at_ends])[0]


def swap(value, axis, mask):
    return lax.ppermute(value, axis, [(i, i ^ mask) for i in range(lax.axis_size(axis))])


def leg(block, first):
    odd, even = (4, 2) if first else (2, 4)
    return lax.ppermute(block, "ctx", [(i, i ^ (odd if i % 2 else even)) for i in range(8)])


def gather(block):
    n_ctx = lax.axis_size("ctx")
    blocks = [block if m == 0 else swap(block, "ctx", m) for m in range(0, n_ctx, 2)]
    return [b for pair in blocks for b in (pair, swap(pair, "ctx", 1))]


def send(value, pairs):
    return lax.ppermute(value, "head", pairs)


def scatter_line(part):
    next_inner, = part((2,))
    first = send(next_inner, [(0, 1), (1, 3), (2, 0), (3, 2)])
    far, = part((3,), next_inner)
    ends = send(far, [(0, 3), (3, 0)])
    near, own = part((1, 0), far)
    near = send(near, [(0, 1), (1, 0), (2, 3), (3, 2)])
    middle = send(add([far, first]), [(1, 2), (2, 1)])
    return add([own, near, ends, middle], [first])


def scatter_direct(part, n_head):
    parts = []
    for x in [*range(n_head - 1, 0, -1), 0]:
        got, = part((x,))
        parts.append(swap(got, "head", x) if x else got)
    return add(parts)


def shards(queries, fresh_keys, fresh_values, cache_keys, cache_values, page_request, prompt_lengths, output_weight):
    n_ctx, n_head = lax.axis_size("ctx"), lax.axis_size("head")
    rows, columns = queries.shape[0], output_weight.shape[1]
    tokens, pages = cache_keys.shape[0], page_request.shape[0]
    kv_width = 2 * fresh_keys.shape[1] // n_head
    q_width = queries.shape[1] // n_head
    groups = kv_width // (2 * HD)
    stacked = q_width // (groups * HD) * rows
    keys = n_ctx * tokens

    *packed, sent = call(
        pack_kernel, [shaped(rows, kv_width)] * n_head + [shaped(tokens + pages, kv_width)],
        [page_request, fresh_keys, fresh_values, cache_keys, cache_values], room=58 * MIB,
    )
    fresh, cache, ends, *query = call(
        stage_kernel,
        [shaped(rows, kv_width), shaped(tokens + pages, kv_width), shaped(prompt_lengths.shape[0], LANES, jnp.int32)]
        + [shaped(rows, q_width)] * n_head,
        [prompt_lengths, queries, packed[0], sent],
    )

    fresh = stack([fresh, *(swap(packed[x], "head", x) for x in range(1, n_head))])
    for x in range(1, n_head):
        query[x] = swap(stack([query[x]], fresh) if x > 1 else query[x], "head", x)
    square = n_ctx == 8 and n_head == 4
    if square:
        pair = stack([cache, leg(sent, True)], fresh)
        far = leg(pair, False)
        got = leg(fresh, True)
        cache = stack([pair, far], got, *query[1:3])
        cache = [cache, swap(cache, "ctx", 1)]
        fresh = stack([fresh, got])
        early, late = [fresh, swap(fresh, "ctx", 1)], [leg(fresh, False)]
    else:
        cache, fresh = gather(sent), gather(fresh)
        early, late = fresh[:n_ctx // 2], fresh[n_ctx // 2:]

    attend_keys = lambda n: dict(
        scratch=[pltpu.VMEM((groups, stacked, n * tokens), F32), pltpu.VMEM((n, tokens, LANES), BF16)],
        room=4 * groups * stacked * n * tokens + 6 * MIB,
    )

    state = {}

    def first(xs, *after):
        n = n_ctx + n_ctx // 2
        found = call(
            functools.partial(first_kernel, xs, len(cache), len(cache) + len(early), n_ctx, n_head, q_width),
            [jax.ShapeDtypeStruct((groups, stacked, lanes), F32) for _ in xs for lanes in (2 * HD, LANES)],
            [ends, *(query[x] for x in xs), *cache, *early], after=after, **attend_keys(n),
            cost=pl.CostEstimate(
                flops=16 * len(xs) * rows * q_width * n * tokens,
                bytes_accessed=2 * n * tokens * kv_width,
                transcendentals=len(xs) * rows * (q_width // HD) * n * tokens,
            ),
        )
        state.update((x, found[2 * i:2 * i + 2]) for i, x in enumerate(xs))

    def part(xs, *after):
        n = n_ctx - n_ctx // 2
        options = attend_keys(n)
        options["scratch"].append(pltpu.VMEM((len(xs) * rows, q_width), BF16))
        return call(
            functools.partial(last_kernel, xs, len(late), n_ctx, n_head, q_width), [shaped(rows, columns)] * len(xs),
            [ends, *(query[x] for x in xs), *late, *(a for x in xs for a in state[x]), output_weight],
            after=after, **options,
            cost=pl.CostEstimate(
                flops=len(xs) * (16 * rows * q_width * n * tokens + 8 * rows * q_width * columns),
                bytes_accessed=2 * n * tokens * kv_width,
                transcendentals=len(xs) * rows * (q_width // HD) * n * tokens,
            ),
        )

    if square:
        first((2,))
        late = [stack(late, state[2][1], query[3])]
        late.append(swap(late[0], "ctx", 1))

    def chunks(xs, *after):
        todo = tuple(x for x in xs if x not in state)
        if todo:
            first(todo, *after)
        return part(xs)

    return scatter_line(chunks) if square else scatter_direct(chunks, n_head)


def solution(mesh):
    placed = (
        P(("ctx", "head"), None),
        P(("ctx", "head"), None),
        P(("ctx", "head"), None),
        P("ctx", "head"),
        P("ctx", "head"),
        P("ctx"),
        P(),
        P("head", None),
    )
    return jax.shard_map(
        shards, mesh=mesh, in_specs=placed, out_specs=P(("ctx", "head"), None), check_vma=False
    )
```

```python
import functools
import math

import jax
import jax.numpy as jnp
from jax import lax
from jax.experimental import pallas as pl
from jax.experimental.pallas import tpu as pltpu
from jax.sharding import PartitionSpec as P

HD = 128
PAGE = 16
LANES = 128
HIDDEN = -1e30
MIB = 1024 * 1024
BF16 = jnp.bfloat16
F32 = jnp.float32


def iota(shape, dim):
    return lax.broadcasted_iota(jnp.int32, shape, dim)


def shaped(rows, columns, dtype=BF16):
    return jax.ShapeDtypeStruct((rows, columns), dtype)


def call(kernel, outs, ins, after=(), scratch=(), room=6 * MIB, cost=None):
    count = len(ins)

    def body(*refs):
        kernel(*refs[:count], *refs[count + len(after):])

    integers = lambda a: a.ndim == 1 and a.dtype == jnp.int32
    specs = [pl.BlockSpec(memory_space=pltpu.SMEM if integers(a) else pltpu.VMEM) for a in ins]
    return pl.pallas_call(
        body,
        out_shape=outs,
        in_specs=specs + [pl.BlockSpec(memory_space=pl.ANY)] * len(after),
        out_specs=[pl.BlockSpec(memory_space=pltpu.VMEM)] * len(outs),
        scratch_shapes=list(scratch),
        compiler_params=pltpu.CompilerParams(vmem_limit_bytes=room),
        cost_estimate=cost,
    )(*ins, *after)


def part_of(ref, index, count):
    width = ref.shape[1] // count
    return ref[:, pl.ds(pl.multiple_of(index * width, width), width)]


def pack_kernel(pages, k_ref, v_ref, ck_ref, cv_ref, *outs):
    *fresh, cache = outs
    head = lax.axis_index("head")
    tokens, width = ck_ref.shape
    for x, out in enumerate(fresh):
        out[:, :width] = part_of(k_ref, head ^ x, len(fresh))
        out[:, width:] = part_of(v_ref, head ^ x, len(fresh))
    cache[:tokens, :width] = ck_ref[...]
    cache[:tokens, width:] = cv_ref[...]
    count = pages.shape[0]
    page = iota((count, 2 * width), 0)
    owner = jnp.zeros((count, 2 * width), jnp.int32)
    for p in range(count):
        owner = jnp.where(page == p, pages[p], owner)
    cache[tokens:, :] = owner.astype(F32).astype(BF16)


def stage_kernel(lengths, q_ref, fresh_ref, cache_ref, fresh, cache, ends, *query):
    head = lax.axis_index("head")
    for x, out in enumerate(query):
        out[...] = part_of(q_ref, head ^ x, len(query))
    fresh[...] = fresh_ref[...]
    cache[...] = cache_ref[...]
    row = iota(ends.shape, 0)
    end, filled = 0, jnp.zeros(ends.shape, jnp.int32)
    for r in range(lengths.shape[0]):
        end = end + lengths[r]
        filled = jnp.where(row == r, end, filled)
    ends[...] = filled


def stack_kernel(*refs):
    out, rows = refs[-1], refs[0].shape[0]
    for i, ref in enumerate(refs[:-1]):
        out[i * rows:(i + 1) * rows, :] = ref[...]


def stack(parts, *after):
    rows, columns = parts[0].shape
    return call(stack_kernel, [shaped(len(parts) * rows, columns)], parts, after=after)[0]


class Layout:
    def __init__(self, ends, rows, q_width, kv_width, n_ctx, n_head):
        self.rows, self.n_ctx, self.n_head = rows, n_ctx, n_head
        self.groups = kv_width // (2 * HD)
        self.repeat = q_width // (self.groups * HD)
        self.half = n_head * rows // 2
        self.c, self.h = lax.axis_index("ctx"), lax.axis_index("head")
        self.ends = [ends[r:r + 1, :] for r in range(ends.shape[0])]
        self.lane = iota((rows, LANES), 1)
        self.row = iota((rows, LANES), 0)
        self.row_lane = self.lane - (LANES - rows)

    def start_of(self, rank, head):
        first = head * self.rows < self.half
        piece = jnp.where(first, rank, 2 * self.n_ctx - 1 - rank)
        return piece * self.half + lax.rem(head * self.rows, self.half)

    def step_of(self, b):
        if self.n_ctx != 8 or self.n_head != 4:
            return b
        near = jnp.where(lax.rem(self.c, 2) == 0, 2, 4)
        return [0, near, 1, 7 - near, 6 - near, 6, 1 + near, 7][b]

    def request(self, position):
        request = jnp.zeros(position.shape, jnp.int32)
        for end in self.ends:
            request += (position >= end).astype(jnp.int32)
        return request

    def query_rows(self, query, x):
        q = query[...]
        own = self.lane == self.request(self.start_of(self.c, self.h ^ x) + self.row)
        mask = jnp.where(own | (self.row_lane == self.row), 1.0, 0.0).astype(BF16)
        result = []
        for g in range(self.groups):
            heads = [
                jnp.concatenate([q[:, n * HD:(n + 1) * HD], mask], axis=1)
                for n in range(g * self.repeat, (g + 1) * self.repeat)
            ]
            result.append(jnp.concatenate(heads, axis=0))
        return result

    def fresh_mask(self, b, head):
        p0 = self.start_of(self.c, head)
        parts = []
        for x in range(self.n_head):
            position = self.start_of(self.c ^ self.step_of(b), self.h ^ x) + self.row
            other = (self.lane < len(self.ends)) & (self.request(position) != self.lane)
            later = (self.row_lane >= 0) & (position > p0 + self.row_lane)
            parts.append(jnp.where(other | later, HIDDEN, 0.0))
        return jnp.concatenate(parts, axis=0).astype(BF16)

    def cache_mask(self, owner):
        pages = owner.shape[0]
        lane = iota((pages, LANES), 1)
        other = (lane < len(self.ends)) & (owner.astype(F32) != lane.astype(F32))
        bias = jnp.where(other, HIDDEN, 0.0)
        bias = jnp.broadcast_to(bias[:, None, :], (pages, PAGE, LANES))
        return bias.reshape(pages * PAGE, LANES).astype(BF16)


def attend(q_rows, blocks, masks, scores, tokens, g, groups):
    scale = math.log2(math.e) / math.sqrt(HD)
    largest = None
    for b, (block, mask) in enumerate(zip(blocks, masks)):
        keys = jnp.concatenate([block[:tokens, g * HD:(g + 1) * HD], mask[...]], axis=1)
        s = lax.dot_general(q_rows, keys, (((1,), (1,)), ((), ())), preferred_element_type=F32)
        scores[:, b * tokens:(b + 1) * tokens] = s
        for t in range(tokens // LANES):
            part = s[:, t * LANES:(t + 1) * LANES]
            largest = part if largest is None else jnp.maximum(largest, part)
    top = jnp.max(largest, axis=1, keepdims=True) * scale
    ones = jnp.ones((tokens, HD), BF16)
    summed = jnp.zeros((q_rows.shape[0], 2 * HD), F32)
    for b, block in enumerate(blocks):
        weights = jnp.exp2(scores[:, b * tokens:(b + 1) * tokens] * scale - top).astype(BF16)
        values = jnp.concatenate([block[:tokens, (groups + g) * HD:(groups + g + 1) * HD], ones], axis=1)
        summed += jnp.dot(weights, values, preferred_element_type=F32)
    return summed, jnp.broadcast_to(top, (q_rows.shape[0], LANES))


def views(refs, tokens):
    return [ref.at[pl.ds(i, tokens)] for ref in refs for i in range(0, ref.shape[0], tokens)]


def first_kernel(xs, cached, count, n_ctx, n_head, q_width, ends, *refs):
    query, refs = refs[:len(xs)], refs[len(xs):]
    outs, (scores, masks) = refs[count:-2], refs[-2:]
    tokens = masks.shape[1]
    cache = views(refs[:cached], tokens + tokens // PAGE)
    fresh = views(refs[cached:count], tokens)
    at = Layout(ends, query[0].shape[0], q_width, cache[0].shape[1], n_ctx, n_head)
    for b in range(n_ctx):
        masks[b] = at.cache_mask(cache[b][tokens:, :LANES])
    for i, x in enumerate(xs):
        summed, tops = outs[2 * i:2 * i + 2]
        for b in range(len(fresh)):
            masks[n_ctx + b] = at.fresh_mask(b, at.h ^ x)
        q_rows = at.query_rows(query[i], x)
        for g in range(at.groups):
            summed[g], tops[g] = attend(
                q_rows[g], cache + fresh, [masks.at[b] for b in range(n_ctx + len(fresh))], scores.at[g], tokens, g, at.groups
            )


def last_kernel(xs, count, n_ctx, n_head, q_width, ends, *refs):
    query, refs = refs[:len(xs)], refs[len(xs):]
    fresh, state, refs = refs[:count], refs[count:count + 2 * len(xs)], refs[count + 2 * len(xs):]
    weight, outs, (scores, masks, mixed) = refs[0], refs[1:-3], refs[-3:]
    rows, tokens = query[0].shape[0], masks.shape[1]
    fresh = views(fresh, tokens)
    at = Layout(ends, rows, q_width, fresh[0].shape[1], n_ctx, n_head)
    for i, x in enumerate(xs):
        summed, tops = state[2 * i:2 * i + 2]
        for b in range(len(fresh)):
            masks[b] = at.fresh_mask(n_ctx - len(fresh) + b, at.h ^ x)
        q_rows = at.query_rows(query[i], x)
        for g in range(at.groups):
            sum_b, top_b = attend(
                q_rows[g], fresh, [masks.at[b] for b in range(len(fresh))], scores.at[g], tokens, g, at.groups
            )
            top = jnp.maximum(tops[g], top_b)
            factor_a, factor_b = jnp.exp2(tops[g] - top), jnp.exp2(top_b - top)
            value = summed[g, :, :HD] * factor_a + sum_b[:, :HD] * factor_b
            total = summed[g, :, HD:] * factor_a + sum_b[:, HD:] * factor_b
            attended = (value / total).astype(BF16)
            for j in range(at.repeat):
                n = g * at.repeat + j
                mixed[i * rows:(i + 1) * rows, n * HD:(n + 1) * HD] = attended[j * rows:(j + 1) * rows]
    width = outs[0].shape[1]
    step = min(1024, width)
    for n in range(width // step):
        columns = slice(n * step, (n + 1) * step)
        y = jnp.dot(mixed[...], weight[:, columns], preferred_element_type=F32).astype(BF16)
        for i, out in enumerate(outs):
            out[:, columns] = y[i * rows:(i + 1) * rows]


def add_kernel(count, *refs):
    out, rest = refs[-1], refs[count:-1]
    total = refs[0][...].astype(F32)
    for ref in refs[1:count]:
        total += ref[...].astype(F32)
    out[...] = total.astype(BF16)
    for ref in rest:
        head = lax.axis_index("head")

        @pl.when((head == 0) | (head == lax.axis_size("head") - 1))
        def _():
            out[...] = (total + ref[...].astype(F32)).astype(BF16)


def add(parts, at_ends=()):
    return call(functools.partial(add_kernel, len(parts)), [shaped(*parts[0].shape)], [*parts, *at_ends])[0]


def swap(value, axis, mask):
    return lax.ppermute(value, axis, [(i, i ^ mask) for i in range(lax.axis_size(axis))])


def leg(block, first):
    odd, even = (4, 2) if first else (2, 4)
    return lax.ppermute(block, "ctx", [(i, i ^ (odd if i % 2 else even)) for i in range(8)])


def gather(block):
    n_ctx = lax.axis_size("ctx")
    blocks = [block if m == 0 else swap(block, "ctx", m) for m in range(0, n_ctx, 2)]
    return [b for pair in blocks for b in (pair, swap(pair, "ctx", 1))]


def send(value, pairs):
    return lax.ppermute(value, "head", pairs)


def scatter_line(part):
    next_inner, = part((2,))
    first = send(next_inner, [(0, 1), (1, 3), (2, 0), (3, 2)])
    far, = part((3,), next_inner)
    ends = send(far, [(0, 3), (3, 0)])
    near, = part((1,), far)
    own, = part((0,), near)
    near = send(near, [(0, 1), (1, 0), (2, 3), (3, 2)])
    middle = send(add([far, first]), [(1, 2), (2, 1)])
    return add([own, near, ends, middle], [first])


def scatter_direct(part, n_head):
    parts = []
    for x in [*range(n_head - 1, 0, -1), 0]:
        got, = part((x,))
        parts.append(swap(got, "head", x) if x else got)
    return add(parts)


def shards(queries, fresh_keys, fresh_values, cache_keys, cache_values, page_request, prompt_lengths, output_weight):
    n_ctx, n_head = lax.axis_size("ctx"), lax.axis_size("head")
    rows, columns = queries.shape[0], output_weight.shape[1]
    tokens, pages = cache_keys.shape[0], page_request.shape[0]
    kv_width = 2 * fresh_keys.shape[1] // n_head
    q_width = queries.shape[1] // n_head
    groups = kv_width // (2 * HD)
    stacked = q_width // (groups * HD) * rows
    keys = n_ctx * tokens

    *packed, sent = call(
        pack_kernel, [shaped(rows, kv_width)] * n_head + [shaped(tokens + pages, kv_width)],
        [page_request, fresh_keys, fresh_values, cache_keys, cache_values], room=58 * MIB,
    )
    fresh, cache, ends, *query = call(
        stage_kernel,
        [shaped(rows, kv_width), shaped(tokens + pages, kv_width), shaped(prompt_lengths.shape[0], LANES, jnp.int32)]
        + [shaped(rows, q_width)] * n_head,
        [prompt_lengths, queries, packed[0], sent],
    )

    fresh = stack([fresh, *(swap(packed[x], "head", x) for x in range(1, n_head))])
    for x in range(1, n_head):
        query[x] = swap(stack([query[x]], fresh) if x > 1 else query[x], "head", x)
    square = n_ctx == 8 and n_head == 4
    if square:
        beside, across = leg(sent, True), leg(sent, False)
        corner = leg(stack([beside], fresh), False)
        got = leg(fresh, True)
        cache = stack([cache, beside, across, corner], got, *query[1:3])
        cache = [cache, swap(cache, "ctx", 1)]
        fresh = stack([fresh, got])
        early, late = [fresh, swap(fresh, "ctx", 1)], [leg(fresh, False)]
    else:
        cache, fresh = gather(sent), gather(fresh)
        early, late = fresh[:n_ctx // 2], fresh[n_ctx // 2:]

    attend_keys = lambda n: dict(
        scratch=[pltpu.VMEM((groups, stacked, n * tokens), F32), pltpu.VMEM((n, tokens, LANES), BF16)],
        room=4 * groups * stacked * n * tokens + 6 * MIB,
    )

    state = {}

    def first(xs, *after):
        n = n_ctx + n_ctx // 2
        found = call(
            functools.partial(first_kernel, xs, len(cache), len(cache) + len(early), n_ctx, n_head, q_width),
            [jax.ShapeDtypeStruct((groups, stacked, lanes), F32) for _ in xs for lanes in (2 * HD, LANES)],
            [ends, *(query[x] for x in xs), *cache, *early], after=after, **attend_keys(n),
            cost=pl.CostEstimate(
                flops=16 * len(xs) * rows * q_width * n * tokens,
                bytes_accessed=2 * n * tokens * kv_width,
                transcendentals=len(xs) * rows * (q_width // HD) * n * tokens,
            ),
        )
        state.update((x, found[2 * i:2 * i + 2]) for i, x in enumerate(xs))

    def part(xs, *after):
        n = n_ctx - n_ctx // 2
        options = attend_keys(n)
        options["scratch"].append(pltpu.VMEM((len(xs) * rows, q_width), BF16))
        return call(
            functools.partial(last_kernel, xs, len(late), n_ctx, n_head, q_width), [shaped(rows, columns)] * len(xs),
            [ends, *(query[x] for x in xs), *late, *(a for x in xs for a in state[x]), output_weight],
            after=after, **options,
            cost=pl.CostEstimate(
                flops=len(xs) * (16 * rows * q_width * n * tokens + 8 * rows * q_width * columns),
                bytes_accessed=2 * n * tokens * kv_width,
                transcendentals=len(xs) * rows * (q_width // HD) * n * tokens,
            ),
        )

    if square:
        first((2,))
        late = [stack(late, state[2][1], query[3])]
        late.append(swap(late[0], "ctx", 1))

    def chunks(xs, *after):
        todo = tuple(x for x in xs if x not in state)
        if todo:
            first(todo, *after)
        return part(xs, *after)

    return scatter_line(chunks) if square else scatter_direct(chunks, n_head)


def solution(mesh):
    placed = (
        P(("ctx", "head"), None),
        P(("ctx", "head"), None),
        P(("ctx", "head"), None),
        P("ctx", "head"),
        P("ctx", "head"),
        P("ctx"),
        P(),
        P("head", None),
    )
    return jax.shard_map(
        shards, mesh=mesh, in_specs=placed, out_specs=P(("ctx", "head"), None), check_vma=False
    )
```

```python
import functools
import math

import jax
import jax.numpy as jnp
from jax import lax
from jax.experimental import pallas as pl
from jax.experimental.pallas import tpu as pltpu
from jax.sharding import PartitionSpec as P

HD = 128
PAGE = 16
LANES = 128
HIDDEN = -1e30
MIB = 1024 * 1024
BF16 = jnp.bfloat16
F32 = jnp.float32


def iota(shape, dim):
    return lax.broadcasted_iota(jnp.int32, shape, dim)


def shaped(rows, columns, dtype=BF16):
    return jax.ShapeDtypeStruct((rows, columns), dtype)


def call(kernel, outs, ins, after=(), scratch=(), room=6 * MIB, cost=None):
    count = len(ins)

    def body(*refs):
        kernel(*refs[:count], *refs[count + len(after):])

    integers = lambda a: a.ndim == 1 and a.dtype == jnp.int32
    specs = [pl.BlockSpec(memory_space=pltpu.SMEM if integers(a) else pltpu.VMEM) for a in ins]
    return pl.pallas_call(
        body,
        out_shape=outs,
        in_specs=specs + [pl.BlockSpec(memory_space=pl.ANY)] * len(after),
        out_specs=[pl.BlockSpec(memory_space=pltpu.VMEM)] * len(outs),
        scratch_shapes=list(scratch),
        compiler_params=pltpu.CompilerParams(vmem_limit_bytes=room),
        cost_estimate=cost,
    )(*ins, *after)


def part_of(ref, index, count):
    width = ref.shape[1] // count
    return ref[:, pl.ds(pl.multiple_of(index * width, width), width)]


def own_rows(rows, q_width, kv_width, block):
    return [0, rows, rows + block, rows + block + rows * q_width // kv_width, 16 + rows + block + rows * q_width // kv_width]


def pack_kernel(n_head, lengths, pages, k_ref, v_ref, q_ref, ck_ref, cv_ref, *outs):
    fresh, query, (cache, own) = outs[:n_head - 1], outs[n_head - 1:-2], outs[-2:]
    head = lax.axis_index("head")
    rows, (tokens, width) = k_ref.shape[0], ck_ref.shape
    kv_width, count = 2 * width, pages.shape[0]
    q_width = q_ref.shape[1] // n_head
    _, own_cache, own_query, own_ends, _ = own_rows(rows, q_width, kv_width, tokens + count)
    page = iota((count, kv_width), 0)
    owner = jnp.zeros((count, kv_width), jnp.int32)
    for p in range(count):
        owner = jnp.where(page == p, pages[p], owner)
    owner = owner.astype(F32).astype(BF16)
    for out, start in ((cache, 0), (own, own_cache)):
        out[start:start + tokens, :width] = ck_ref[...]
        out[start:start + tokens, width:] = cv_ref[...]
        out[start + tokens:start + tokens + count, :] = owner
    for x, out in enumerate([own, *fresh]):
        out[:rows, :width] = part_of(k_ref, head ^ x, n_head)
        out[:rows, width:] = part_of(v_ref, head ^ x, n_head)
    for x, out in enumerate(query, 1):
        out[...] = part_of(q_ref, head ^ x, n_head)
    mine = part_of(q_ref, head, n_head)
    for i in range(q_width // kv_width):
        own[own_query + i * rows:own_query + (i + 1) * rows, :] = mine[:, i * kv_width:(i + 1) * kv_width]
    row, low = iota((16, kv_width), 0), iota((16, kv_width), 1) >= LANES
    end, filled = 0, jnp.zeros((16, kv_width), jnp.int32)
    for r in range(lengths.shape[0]):
        end = end + lengths[r]
        filled = jnp.where(row == r, jnp.where(low, end & 127, end >> 7), filled)
    own[own_ends:, :] = filled.astype(F32).astype(BF16)


def stage_kernel(own, fresh, cache, ends, query):
    rows, q_width = query.shape
    block, kv_width = cache.shape
    _, own_cache, own_query, own_ends, _ = own_rows(rows, q_width, kv_width, block)
    fresh[...] = own[:rows, :]
    cache[...] = own[own_cache:own_query, :]
    for i in range(q_width // kv_width):
        query[:, i * kv_width:(i + 1) * kv_width] = own[own_query + i * rows:own_query + (i + 1) * rows, :]
    digits = own[own_ends:, :].astype(F32).astype(jnp.int32)
    ends[...] = (digits[:, :LANES] * 128 + digits[:, LANES:2 * LANES])[:ends.shape[0]]


def stack_kernel(*refs):
    out, rows = refs[-1], refs[0].shape[0]
    for i, ref in enumerate(refs[:-1]):
        out[i * rows:(i + 1) * rows, :] = ref[...]


def stack(parts, *after):
    rows, columns = parts[0].shape
    return call(stack_kernel, [shaped(len(parts) * rows, columns)], parts, after=after)[0]


class Layout:
    def __init__(self, ends, rows, q_width, kv_width, n_ctx, n_head):
        self.rows, self.n_ctx, self.n_head = rows, n_ctx, n_head
        self.groups = kv_width // (2 * HD)
        self.repeat = q_width // (self.groups * HD)
        self.half = n_head * rows // 2
        self.c, self.h = lax.axis_index("ctx"), lax.axis_index("head")
        self.ends = [ends[r:r + 1, :] for r in range(ends.shape[0])]
        self.lane = iota((rows, LANES), 1)
        self.row = iota((rows, LANES), 0)
        self.row_lane = self.lane - (LANES - rows)

    def start_of(self, rank, head):
        first = head * self.rows < self.half
        piece = jnp.where(first, rank, 2 * self.n_ctx - 1 - rank)
        return piece * self.half + lax.rem(head * self.rows, self.half)

    def step_of(self, b):
        if self.n_ctx != 8 or self.n_head != 4:
            return b
        near = jnp.where(lax.rem(self.c, 2) == 0, 2, 4)
        return [0, near, 1, 7 - near, 6 - near, 6, 1 + near, 7][b]

    def request(self, position):
        request = jnp.zeros(position.shape, jnp.int32)
        for end in self.ends:
            request += (position >= end).astype(jnp.int32)
        return request

    def query_rows(self, query, x):
        q = query[...]
        own = self.lane == self.request(self.start_of(self.c, self.h ^ x) + self.row)
        mask = jnp.where(own | (self.row_lane == self.row), 1.0, 0.0).astype(BF16)
        result = []
        for g in range(self.groups):
            heads = [
                jnp.concatenate([q[:, n * HD:(n + 1) * HD], mask], axis=1)
                for n in range(g * self.repeat, (g + 1) * self.repeat)
            ]
            result.append(jnp.concatenate(heads, axis=0))
        return result

    def fresh_mask(self, b, head):
        p0 = self.start_of(self.c, head)
        parts = []
        for x in [0, *range(self.n_head - 1, 0, -1)]:
            position = self.start_of(self.c ^ self.step_of(b), self.h ^ x) + self.row
            other = (self.lane < len(self.ends)) & (self.request(position) != self.lane)
            later = (self.row_lane >= 0) & (position > p0 + self.row_lane)
            parts.append(jnp.where(other | later, HIDDEN, 0.0))
        return jnp.concatenate(parts, axis=0).astype(BF16)

    def cache_mask(self, owner):
        pages = owner.shape[0]
        lane = iota((pages, LANES), 1)
        other = (lane < len(self.ends)) & (owner.astype(F32) != lane.astype(F32))
        bias = jnp.where(other, HIDDEN, 0.0)
        bias = jnp.broadcast_to(bias[:, None, :], (pages, PAGE, LANES))
        return bias.reshape(pages * PAGE, LANES).astype(BF16)


def attend(q_rows, blocks, masks, scores, tokens, g, groups):
    scale = math.log2(math.e) / math.sqrt(HD)
    largest = None
    for b, (block, mask) in enumerate(zip(blocks, masks)):
        keys = jnp.concatenate([block[:tokens, g * HD:(g + 1) * HD], mask[...]], axis=1)
        s = lax.dot_general(q_rows, keys, (((1,), (1,)), ((), ())), preferred_element_type=F32)
        scores[:, b * tokens:(b + 1) * tokens] = s
        for t in range(tokens // LANES):
            part = s[:, t * LANES:(t + 1) * LANES]
            largest = part if largest is None else jnp.maximum(largest, part)
    top = jnp.max(largest, axis=1, keepdims=True) * scale
    ones = jnp.ones((tokens, HD), BF16)
    summed = jnp.zeros((q_rows.shape[0], 2 * HD), F32)
    for b, block in enumerate(blocks):
        weights = jnp.exp2(scores[:, b * tokens:(b + 1) * tokens] * scale - top).astype(BF16)
        values = jnp.concatenate([block[:tokens, (groups + g) * HD:(groups + g + 1) * HD], ones], axis=1)
        summed += jnp.dot(weights, values, preferred_element_type=F32)
    return summed, jnp.broadcast_to(top, (q_rows.shape[0], LANES))


def views(refs, tokens):
    return [ref.at[pl.ds(i, tokens)] for ref in refs for i in range(0, ref.shape[0], tokens)]


def first_kernel(xs, cached, count, n_ctx, n_head, q_width, ends, *refs):
    query, refs = refs[:len(xs)], refs[len(xs):]
    outs, (scores, masks) = refs[count:-2], refs[-2:]
    tokens = masks.shape[1]
    cache = views(refs[:cached], tokens + tokens // PAGE)
    fresh = views(refs[cached:count], tokens)
    at = Layout(ends, query[0].shape[0], q_width, cache[0].shape[1], n_ctx, n_head)
    for b in range(n_ctx):
        masks[b] = at.cache_mask(cache[b][tokens:, :LANES])
    for i, x in enumerate(xs):
        summed, tops = outs[2 * i:2 * i + 2]
        for b in range(len(fresh)):
            masks[n_ctx + b] = at.fresh_mask(b, at.h ^ x)
        q_rows = at.query_rows(query[i], x)
        for g in range(at.groups):
            summed[g], tops[g] = attend(
                q_rows[g], cache + fresh, [masks.at[b] for b in range(n_ctx + len(fresh))], scores.at[g], tokens, g, at.groups
            )


def last_kernel(xs, count, n_ctx, n_head, q_width, ends, *refs):
    query, refs = refs[:len(xs)], refs[len(xs):]
    fresh, state, refs = refs[:count], refs[count:count + 2 * len(xs)], refs[count + 2 * len(xs):]
    weight, outs, (scores, masks, mixed) = refs[0], refs[1:-3], refs[-3:]
    rows, tokens = query[0].shape[0], masks.shape[1]
    fresh = views(fresh, tokens)
    at = Layout(ends, rows, q_width, fresh[0].shape[1], n_ctx, n_head)
    for i, x in enumerate(xs):
        summed, tops = state[2 * i:2 * i + 2]
        for b in range(len(fresh)):
            masks[b] = at.fresh_mask(n_ctx - len(fresh) + b, at.h ^ x)
        q_rows = at.query_rows(query[i], x)
        for g in range(at.groups):
            sum_b, top_b = attend(
                q_rows[g], fresh, [masks.at[b] for b in range(len(fresh))], scores.at[g], tokens, g, at.groups
            )
            top = jnp.maximum(tops[g], top_b)
            factor_a, factor_b = jnp.exp2(tops[g] - top), jnp.exp2(top_b - top)
            value = summed[g, :, :HD] * factor_a + sum_b[:, :HD] * factor_b
            total = summed[g, :, HD:] * factor_a + sum_b[:, HD:] * factor_b
            attended = (value / total).astype(BF16)
            for j in range(at.repeat):
                n = g * at.repeat + j
                mixed[i * rows:(i + 1) * rows, n * HD:(n + 1) * HD] = attended[j * rows:(j + 1) * rows]
    width = outs[0].shape[1]
    step = min(1024, width)
    for n in range(width // step):
        columns = slice(n * step, (n + 1) * step)
        y = jnp.dot(mixed[...], weight[:, columns], preferred_element_type=F32).astype(BF16)
        for i, out in enumerate(outs):
            out[:, columns] = y[i * rows:(i + 1) * rows]


def add_kernel(count, *refs):
    out, rest = refs[-1], refs[count:-1]
    total = refs[0][...].astype(F32)
    for ref in refs[1:count]:
        total += ref[...].astype(F32)
    out[...] = total.astype(BF16)
    for ref in rest:
        head = lax.axis_index("head")

        @pl.when((head == 0) | (head == lax.axis_size("head") - 1))
        def _():
            out[...] = (total + ref[...].astype(F32)).astype(BF16)


def add(parts, at_ends=()):
    return call(functools.partial(add_kernel, len(parts)), [shaped(*parts[0].shape)], [*parts, *at_ends])[0]


def swap(value, axis, mask):
    return lax.ppermute(value, axis, [(i, i ^ mask) for i in range(lax.axis_size(axis))])


def leg(block, first):
    odd, even = (4, 2) if first else (2, 4)
    return lax.ppermute(block, "ctx", [(i, i ^ (odd if i % 2 else even)) for i in range(8)])


def gather(block):
    n_ctx = lax.axis_size("ctx")
    blocks = [block if m == 0 else swap(block, "ctx", m) for m in range(0, n_ctx, 2)]
    return [b for pair in blocks for b in (pair, swap(pair, "ctx", 1))]


def send(value, pairs):
    return lax.ppermute(value, "head", pairs)


def scatter_line(part):
    next_inner, = part((2,))
    first = send(next_inner, [(0, 1), (1, 3), (2, 0), (3, 2)])
    far, = part((3,), next_inner)
    ends = send(far, [(0, 3), (3, 0)])
    near, = part((1,), far)
    own, = part((0,), near)
    near = send(near, [(0, 1), (1, 0), (2, 3), (3, 2)])
    middle = send(add([far, first]), [(1, 2), (2, 1)])
    return add([own, near, ends, middle], [first])


def scatter_direct(part, n_head):
    parts = []
    for x in [*range(n_head - 1, 0, -1), 0]:
        got, = part((x,))
        parts.append(swap(got, "head", x) if x else got)
    return add(parts)


def shards(queries, fresh_keys, fresh_values, cache_keys, cache_values, page_request, prompt_lengths, output_weight):
    n_ctx, n_head = lax.axis_size("ctx"), lax.axis_size("head")
    rows, columns = queries.shape[0], output_weight.shape[1]
    tokens, pages = cache_keys.shape[0], page_request.shape[0]
    kv_width = 2 * fresh_keys.shape[1] // n_head
    q_width = queries.shape[1] // n_head
    groups = kv_width // (2 * HD)
    stacked = q_width // (groups * HD) * rows
    keys = n_ctx * tokens

    own = shaped(own_rows(rows, q_width, kv_width, tokens + pages)[-1], kv_width)
    *packed, sent, own = call(
        functools.partial(pack_kernel, n_head),
        [shaped(rows, kv_width)] * (n_head - 1) + [shaped(rows, q_width)] * (n_head - 1) + [shaped(tokens + pages, kv_width), own],
        [prompt_lengths, page_request, fresh_keys, fresh_values, queries, cache_keys, cache_values], room=58 * MIB,
    )
    fresh, cache, ends, *query = call(
        stage_kernel,
        [shaped(rows, kv_width), shaped(tokens + pages, kv_width), shaped(prompt_lengths.shape[0], LANES, jnp.int32)]
        + [shaped(rows, q_width)],
        [own],
    )
    query += packed[n_head - 1:]

    fresh = stack([fresh, *(swap(packed[x - 1], "head", x) for x in range(n_head - 1, 0, -1))])
    for x in range(1, n_head):
        query[x] = swap(query[x], "head", x)
    square = n_ctx == 8 and n_head == 4
    if square:
        beside, across = leg(sent, True), leg(sent, False)
        corner = leg(stack([beside], fresh), False)
        got = leg(fresh, True)
        cache = stack([cache, beside, across, corner], got, *query[1:3])
        cache = [cache, swap(cache, "ctx", 1)]
        fresh = stack([fresh, got])
        early, late = [fresh, swap(fresh, "ctx", 1)], [leg(fresh, False)]
    else:
        cache, fresh = gather(sent), gather(fresh)
        early, late = fresh[:n_ctx // 2], fresh[n_ctx // 2:]

    attend_keys = lambda n: dict(
        scratch=[pltpu.VMEM((groups, stacked, n * tokens), F32), pltpu.VMEM((n, tokens, LANES), BF16)],
        room=4 * groups * stacked * n * tokens + 6 * MIB,
    )

    state = {}

    def first(xs, *after):
        n = n_ctx + n_ctx // 2
        found = call(
            functools.partial(first_kernel, xs, len(cache), len(cache) + len(early), n_ctx, n_head, q_width),
            [jax.ShapeDtypeStruct((groups, stacked, lanes), F32) for _ in xs for lanes in (2 * HD, LANES)],
            [ends, *(query[x] for x in xs), *cache, *early], after=after, **attend_keys(n),
            cost=pl.CostEstimate(
                flops=16 * len(xs) * rows * q_width * n * tokens,
                bytes_accessed=2 * n * tokens * kv_width,
                transcendentals=len(xs) * rows * (q_width // HD) * n * tokens,
            ),
        )
        state.update((x, found[2 * i:2 * i + 2]) for i, x in enumerate(xs))

    def part(xs, *after):
        n = n_ctx - n_ctx // 2
        options = attend_keys(n)
        options["scratch"].append(pltpu.VMEM((len(xs) * rows, q_width), BF16))
        return call(
            functools.partial(last_kernel, xs, len(late), n_ctx, n_head, q_width), [shaped(rows, columns)] * len(xs),
            [ends, *(query[x] for x in xs), *late, *(a for x in xs for a in state[x]), output_weight],
            after=after, **options,
            cost=pl.CostEstimate(
                flops=len(xs) * (16 * rows * q_width * n * tokens + 8 * rows * q_width * columns),
                bytes_accessed=2 * n * tokens * kv_width,
                transcendentals=len(xs) * rows * (q_width // HD) * n * tokens,
            ),
        )

    if square:
        first((2,))
        late = [stack(late, state[2][1], query[3])]
        late.append(swap(late[0], "ctx", 1))

    def chunks(xs, *after):
        todo = tuple(x for x in xs if x not in state)
        if todo:
            first(todo, *after)
        return part(xs, *after)

    return scatter_line(chunks) if square else scatter_direct(chunks, n_head)


def solution(mesh):
    placed = (
        P(("ctx", "head"), None),
        P(("ctx", "head"), None),
        P(("ctx", "head"), None),
        P("ctx", "head"),
        P("ctx", "head"),
        P("ctx"),
        P(),
        P("head", None),
    )
    return jax.shard_map(
        shards, mesh=mesh, in_specs=placed, out_specs=P(("ctx", "head"), None), check_vma=False
    )
```

```python
import functools
import math

import jax
import jax.numpy as jnp
from jax import lax
from jax.experimental import pallas as pl
from jax.experimental.pallas import tpu as pltpu
from jax.sharding import PartitionSpec as P

HD = 128
PAGE = 16
LANES = 128
HIDDEN = -1e30
MIB = 1024 * 1024
BF16 = jnp.bfloat16
F32 = jnp.float32


def iota(shape, dim):
    return lax.broadcasted_iota(jnp.int32, shape, dim)


def shaped(rows, columns, dtype=BF16):
    return jax.ShapeDtypeStruct((rows, columns), dtype)


def call(kernel, outs, ins, after=(), scratch=(), room=6 * MIB, cost=None):
    count = len(ins)

    def body(*refs):
        kernel(*refs[:count], *refs[count + len(after):])

    integers = lambda a: a.ndim == 1 and a.dtype == jnp.int32
    specs = [pl.BlockSpec(memory_space=pltpu.SMEM if integers(a) else pltpu.VMEM) for a in ins]
    return pl.pallas_call(
        body,
        out_shape=outs,
        in_specs=specs + [pl.BlockSpec(memory_space=pl.ANY)] * len(after),
        out_specs=[pl.BlockSpec(memory_space=pltpu.VMEM)] * len(outs),
        scratch_shapes=list(scratch),
        compiler_params=pltpu.CompilerParams(vmem_limit_bytes=room),
        cost_estimate=cost,
    )(*ins, *after)


def part_of(ref, index, count):
    width = ref.shape[1] // count
    return ref[:, pl.ds(pl.multiple_of(index * width, width), width)]


def own_rows(rows, q_width, kv_width, block):
    return [0, rows, rows + block, rows + block + rows * q_width // kv_width, 16 + rows + block + rows * q_width // kv_width]


def pack_kernel(n_head, lengths, pages, k_ref, v_ref, q_ref, ck_ref, cv_ref, *outs):
    fresh, query, (cache, own) = outs[:n_head - 1], outs[n_head - 1:-2], outs[-2:]
    head = lax.axis_index("head")
    rows, (tokens, width) = k_ref.shape[0], ck_ref.shape
    kv_width, count = 2 * width, pages.shape[0]
    q_width = q_ref.shape[1] // n_head
    _, own_cache, own_query, own_ends, _ = own_rows(rows, q_width, kv_width, tokens + count)
    page = iota((count, kv_width), 0)
    owner = jnp.zeros((count, kv_width), jnp.int32)
    for p in range(count):
        owner = jnp.where(page == p, pages[p], owner)
    owner = owner.astype(F32).astype(BF16)
    for out, start in ((cache, 0), (own, own_cache)):
        out[start:start + tokens, :width] = ck_ref[...]
        out[start:start + tokens, width:] = cv_ref[...]
        out[start + tokens:start + tokens + count, :] = owner
    for x, out in enumerate([own, *fresh]):
        out[:rows, :width] = part_of(k_ref, head ^ x, n_head)
        out[:rows, width:] = part_of(v_ref, head ^ x, n_head)
    for x, out in enumerate(query, 1):
        out[...] = part_of(q_ref, head ^ x, n_head)
    mine = part_of(q_ref, head, n_head)
    for i in range(q_width // kv_width):
        own[own_query + i * rows:own_query + (i + 1) * rows, :] = mine[:, i * kv_width:(i + 1) * kv_width]
    row, low = iota((16, kv_width), 0), iota((16, kv_width), 1) >= LANES
    end, filled = 0, jnp.zeros((16, kv_width), jnp.int32)
    for r in range(lengths.shape[0]):
        end = end + lengths[r]
        filled = jnp.where(row == r, jnp.where(low, end & 127, end >> 7), filled)
    own[own_ends:, :] = filled.astype(F32).astype(BF16)


def stage_kernel(own, fresh, cache, ends, query):
    rows, q_width = query.shape
    block, kv_width = cache.shape
    _, own_cache, own_query, own_ends, _ = own_rows(rows, q_width, kv_width, block)
    fresh[...] = own[:rows, :]
    cache[...] = own[own_cache:own_query, :]
    for i in range(q_width // kv_width):
        query[:, i * kv_width:(i + 1) * kv_width] = own[own_query + i * rows:own_query + (i + 1) * rows, :]
    digits = own[own_ends:, :].astype(F32).astype(jnp.int32)
    ends[...] = (digits[:, :LANES] * 128 + digits[:, LANES:2 * LANES])[:ends.shape[0]]


def stack_kernel(*refs):
    out, rows = refs[-1], refs[0].shape[0]
    for i, ref in enumerate(refs[:-1]):
        out[i * rows:(i + 1) * rows, :] = ref[...]


def stack(parts, *after):
    rows, columns = parts[0].shape
    return call(stack_kernel, [shaped(len(parts) * rows, columns)], parts, after=after)[0]


class Layout:
    def __init__(self, ends, rows, q_width, kv_width, n_ctx, n_head):
        self.rows, self.n_ctx, self.n_head = rows, n_ctx, n_head
        self.groups = kv_width // (2 * HD)
        self.repeat = q_width // (self.groups * HD)
        self.half = n_head * rows // 2
        self.c, self.h = lax.axis_index("ctx"), lax.axis_index("head")
        self.ends = [ends[r:r + 1, :] for r in range(ends.shape[0])]
        self.lane = iota((rows, LANES), 1)
        self.row = iota((rows, LANES), 0)
        self.row_lane = self.lane - (LANES - rows)

    def start_of(self, rank, head):
        first = head * self.rows < self.half
        piece = jnp.where(first, rank, 2 * self.n_ctx - 1 - rank)
        return piece * self.half + lax.rem(head * self.rows, self.half)

    def step_of(self, b):
        if self.n_ctx != 8 or self.n_head != 4:
            return b
        near = jnp.where(lax.rem(self.c, 2) == 0, 2, 4)
        return [0, near, 1, 7 - near, 6 - near, 6, 1 + near, 7][b]

    def request(self, position):
        request = jnp.zeros(position.shape, jnp.int32)
        for end in self.ends:
            request += (position >= end).astype(jnp.int32)
        return request

    def query_rows(self, query, x):
        q = query[...]
        own = self.lane == self.request(self.start_of(self.c, self.h ^ x) + self.row)
        mask = jnp.where(own | (self.row_lane == self.row), 1.0, 0.0).astype(BF16)
        result = []
        for g in range(self.groups):
            heads = [
                jnp.concatenate([q[:, n * HD:(n + 1) * HD], mask], axis=1)
                for n in range(g * self.repeat, (g + 1) * self.repeat)
            ]
            result.append(jnp.concatenate(heads, axis=0))
        return result

    def fresh_mask(self, b, head):
        p0 = self.start_of(self.c, head)
        parts = []
        for x in [0, *range(self.n_head - 1, 0, -1)]:
            position = self.start_of(self.c ^ self.step_of(b), self.h ^ x) + self.row
            other = (self.lane < len(self.ends)) & (self.request(position) != self.lane)
            later = (self.row_lane >= 0) & (position > p0 + self.row_lane)
            parts.append(jnp.where(other | later, HIDDEN, 0.0))
        return jnp.concatenate(parts, axis=0).astype(BF16)

    def cache_mask(self, owner):
        pages = owner.shape[0]
        lane = iota((pages, LANES), 1)
        other = (lane < len(self.ends)) & (owner.astype(F32) != lane.astype(F32))
        bias = jnp.where(other, HIDDEN, 0.0)
        bias = jnp.broadcast_to(bias[:, None, :], (pages, PAGE, LANES))
        return bias.reshape(pages * PAGE, LANES).astype(BF16)


def attend(q_rows, blocks, masks, scores, tokens, g, groups):
    scale = math.log2(math.e) / math.sqrt(HD)
    largest = None
    for b, (block, mask) in enumerate(zip(blocks, masks)):
        keys = jnp.concatenate([block[:tokens, g * HD:(g + 1) * HD], mask[...]], axis=1)
        s = lax.dot_general(q_rows, keys, (((1,), (1,)), ((), ())), preferred_element_type=F32)
        scores[:, b * tokens:(b + 1) * tokens] = s
        for t in range(tokens // LANES):
            part = s[:, t * LANES:(t + 1) * LANES]
            largest = part if largest is None else jnp.maximum(largest, part)
    top = jnp.max(largest, axis=1, keepdims=True) * scale
    ones = jnp.ones((tokens, HD), BF16)
    summed = jnp.zeros((q_rows.shape[0], 2 * HD), F32)
    for b, block in enumerate(blocks):
        weights = jnp.exp2(scores[:, b * tokens:(b + 1) * tokens] * scale - top).astype(BF16)
        values = jnp.concatenate([block[:tokens, (groups + g) * HD:(groups + g + 1) * HD], ones], axis=1)
        summed += jnp.dot(weights, values, preferred_element_type=F32)
    return summed, jnp.broadcast_to(top, (q_rows.shape[0], LANES))


def views(refs, tokens):
    return [ref.at[pl.ds(i, tokens)] for ref in refs for i in range(0, ref.shape[0], tokens)]


def first_kernel(xs, cached, count, skip, n_ctx, n_head, q_width, ends, *refs):
    query, refs = refs[:len(xs)], refs[len(xs):]
    outs, (scores, masks) = refs[count:-2], refs[-2:]
    tokens = masks.shape[1]
    cache = views(refs[:cached], tokens + tokens // PAGE)
    fresh = views(refs[cached:count], tokens)
    at = Layout(ends, query[0].shape[0], q_width, refs[0].shape[1], n_ctx, n_head)
    blocks = cache + fresh
    for b in range(len(cache)):
        masks[b] = at.cache_mask(cache[b][tokens:, :LANES])
    for i, x in enumerate(xs):
        summed, tops = outs[2 * i:2 * i + 2]
        for b in range(len(fresh)):
            masks[len(cache) + b] = at.fresh_mask(skip + b, at.h ^ x)
        q_rows = at.query_rows(query[i], x)
        for g in range(at.groups):
            summed[g], tops[g] = attend(
                q_rows[g], blocks, [masks.at[b] for b in range(len(blocks))], scores.at[g], tokens, g, at.groups
            )


def last_kernel(xs, count, states, n_ctx, n_head, q_width, ends, *refs):
    query, refs = refs[:len(xs)], refs[len(xs):]
    split = count + 2 * states * len(xs)
    fresh, state, refs = refs[:count], refs[count:split], refs[split:]
    weight, outs, (scores, masks, mixed) = refs[0], refs[1:-3], refs[-3:]
    rows, tokens = query[0].shape[0], masks.shape[1]
    fresh = views(fresh, tokens)
    at = Layout(ends, rows, q_width, fresh[0].shape[1], n_ctx, n_head)
    for i, x in enumerate(xs):
        earlier = state[2 * states * i:2 * states * (i + 1)]
        for b in range(len(fresh)):
            masks[b] = at.fresh_mask(n_ctx - len(fresh) + b, at.h ^ x)
        q_rows = at.query_rows(query[i], x)
        for g in range(at.groups):
            sum_b, top_b = attend(
                q_rows[g], fresh, [masks.at[b] for b in range(len(fresh))], scores.at[g], tokens, g, at.groups
            )
            top = top_b
            for tops in earlier[1::2]:
                top = jnp.maximum(top, tops[g])
            joined = sum_b * jnp.concatenate([jnp.exp2(top_b - top)] * 2, axis=1)
            for summed, tops in zip(earlier[::2], earlier[1::2]):
                joined += summed[g] * jnp.concatenate([jnp.exp2(tops[g] - top)] * 2, axis=1)
            value, total = joined[:, :HD], joined[:, HD:]
            attended = (value / total).astype(BF16)
            for j in range(at.repeat):
                n = g * at.repeat + j
                mixed[i * rows:(i + 1) * rows, n * HD:(n + 1) * HD] = attended[j * rows:(j + 1) * rows]
    width = outs[0].shape[1]
    step = min(1024, width)
    for n in range(width // step):
        columns = slice(n * step, (n + 1) * step)
        y = jnp.dot(mixed[...], weight[:, columns], preferred_element_type=F32).astype(BF16)
        for i, out in enumerate(outs):
            out[:, columns] = y[i * rows:(i + 1) * rows]


def add_kernel(count, *refs):
    out, rest = refs[-1], refs[count:-1]
    total = refs[0][...].astype(F32)
    for ref in refs[1:count]:
        total += ref[...].astype(F32)
    out[...] = total.astype(BF16)
    for ref in rest:
        head = lax.axis_index("head")

        @pl.when((head == 0) | (head == lax.axis_size("head") - 1))
        def _():
            out[...] = (total + ref[...].astype(F32)).astype(BF16)


def add(parts, at_ends=()):
    return call(functools.partial(add_kernel, len(parts)), [shaped(*parts[0].shape)], [*parts, *at_ends])[0]


def swap(value, axis, mask):
    return lax.ppermute(value, axis, [(i, i ^ mask) for i in range(lax.axis_size(axis))])


def leg(block, first):
    odd, even = (4, 2) if first else (2, 4)
    return lax.ppermute(block, "ctx", [(i, i ^ (odd if i % 2 else even)) for i in range(8)])


def gather(block):
    n_ctx = lax.axis_size("ctx")
    blocks = [block if m == 0 else swap(block, "ctx", m) for m in range(0, n_ctx, 2)]
    return [b for pair in blocks for b in (pair, swap(pair, "ctx", 1))]


def send(value, pairs):
    return lax.ppermute(value, "head", pairs)


def scatter_line(part):
    next_inner, = part((2,))
    first = send(next_inner, [(0, 1), (1, 3), (2, 0), (3, 2)])
    far, = part((3,), next_inner)
    ends = send(far, [(0, 3), (3, 0)])
    near, = part((1,), far)
    own, = part((0,), near)
    near = send(near, [(0, 1), (1, 0), (2, 3), (3, 2)])
    middle = send(add([far, first]), [(1, 2), (2, 1)])
    return add([own, near, ends, middle], [first])


def scatter_direct(part, n_head):
    parts = []
    for x in [*range(n_head - 1, 0, -1), 0]:
        got, = part((x,))
        parts.append(swap(got, "head", x) if x else got)
    return add(parts)


def shards(queries, fresh_keys, fresh_values, cache_keys, cache_values, page_request, prompt_lengths, output_weight):
    n_ctx, n_head = lax.axis_size("ctx"), lax.axis_size("head")
    rows, columns = queries.shape[0], output_weight.shape[1]
    tokens, pages = cache_keys.shape[0], page_request.shape[0]
    kv_width = 2 * fresh_keys.shape[1] // n_head
    q_width = queries.shape[1] // n_head
    groups = kv_width // (2 * HD)
    stacked = q_width // (groups * HD) * rows
    keys = n_ctx * tokens

    own = shaped(own_rows(rows, q_width, kv_width, tokens + pages)[-1], kv_width)
    *packed, sent, own = call(
        functools.partial(pack_kernel, n_head),
        [shaped(rows, kv_width)] * (n_head - 1) + [shaped(rows, q_width)] * (n_head - 1) + [shaped(tokens + pages, kv_width), own],
        [prompt_lengths, page_request, fresh_keys, fresh_values, queries, cache_keys, cache_values], room=58 * MIB,
    )
    fresh, cache, ends, *query = call(
        stage_kernel,
        [shaped(rows, kv_width), shaped(tokens + pages, kv_width), shaped(prompt_lengths.shape[0], LANES, jnp.int32)]
        + [shaped(rows, q_width)],
        [own],
    )
    query += packed[n_head - 1:]

    fresh = stack([fresh, *(swap(packed[x - 1], "head", x) for x in range(n_head - 1, 0, -1))])
    for x in range(1, n_head):
        query[x] = swap(query[x], "head", x)
    square = n_ctx == 8 and n_head == 4
    if square:
        beside, across = leg(sent, True), leg(sent, False)
        corner = leg(stack([beside], fresh), False)
        got = leg(fresh, True)
        cache = stack([cache, beside, across, corner], got, *query[1:3])
        cache = [cache, swap(cache, "ctx", 1)]
        fresh = stack([fresh, got])
        early, late = [fresh, swap(fresh, "ctx", 1)], [leg(fresh, False)]
    else:
        cache, fresh = gather(sent), gather(fresh)
        early, late = fresh[:n_ctx // 2], fresh[n_ctx // 2:]

    attend_keys = lambda n: dict(
        scratch=[pltpu.VMEM((groups, stacked, n * tokens), F32), pltpu.VMEM((n, tokens, LANES), BF16)],
        room=4 * groups * stacked * n * tokens + 6 * MIB,
    )

    state = {}

    def first(xs, *after):
        n = n_ctx + n_ctx // 2
        found = call(
            functools.partial(first_kernel, xs, len(cache), len(cache) + len(early), 0, n_ctx, n_head, q_width),
            [jax.ShapeDtypeStruct((groups, stacked, lanes), F32) for _ in xs for lanes in (2 * HD, LANES)],
            [ends, *(query[x] for x in xs), *cache, *early], after=after, **attend_keys(n),
            cost=pl.CostEstimate(
                flops=16 * len(xs) * rows * q_width * n * tokens,
                bytes_accessed=2 * n * tokens * kv_width,
                transcendentals=len(xs) * rows * (q_width // HD) * n * tokens,
            ),
        )
        state.update((x, found[2 * i:2 * i + 2]) for i, x in enumerate(xs))

    def part(xs, *after):
        states = len(state[xs[0]]) // 2
        blocks = late[states - 1:]
        n = sum(block.shape[0] for block in blocks) // tokens
        options = attend_keys(n)
        options["scratch"].append(pltpu.VMEM((len(xs) * rows, q_width), BF16))
        return call(
            functools.partial(last_kernel, xs, len(blocks), states, n_ctx, n_head, q_width), [shaped(rows, columns)] * len(xs),
            [ends, *(query[x] for x in xs), *blocks, *(a for x in xs for a in state[x]), output_weight],
            after=after, **options,
            cost=pl.CostEstimate(
                flops=len(xs) * (16 * rows * q_width * n * tokens + 8 * rows * q_width * columns),
                bytes_accessed=2 * n * tokens * kv_width,
                transcendentals=len(xs) * rows * (q_width // HD) * n * tokens,
            ),
        )

    if square:
        first((2,))
        late = [stack(late, state[2][1], query[3])]
        late.append(swap(late[0], "ctx", 1))
        n = late[0].shape[0] // tokens
        state[2] = state[2] + call(
            functools.partial(first_kernel, (2,), 0, 1, n_ctx - 2 * n, n_ctx, n_head, q_width),
            [jax.ShapeDtypeStruct((groups, stacked, lanes), F32) for lanes in (2 * HD, LANES)],
            [ends, query[2], late[0]], **attend_keys(n),
        )

    def chunks(xs, *after):
        todo = tuple(x for x in xs if x not in state)
        if todo:
            first(todo, *after)
        return part(xs, *after)

    return scatter_line(chunks) if square else scatter_direct(chunks, n_head)


def solution(mesh):
    placed = (
        P(("ctx", "head"), None),
        P(("ctx", "head"), None),
        P(("ctx", "head"), None),
        P("ctx", "head"),
        P("ctx", "head"),
        P("ctx"),
        P(),
        P("head", None),
    )
    return jax.shard_map(
        shards, mesh=mesh, in_specs=placed, out_specs=P(("ctx", "head"), None), check_vma=False
    )
```

```python
import functools
import math

import jax
import jax.numpy as jnp
from jax import lax
from jax.experimental import pallas as pl
from jax.experimental.pallas import tpu as pltpu
from jax.sharding import PartitionSpec as P

HD = 128
PAGE = 16
LANES = 128
HIDDEN = -1e30
MIB = 1024 * 1024
BF16 = jnp.bfloat16
F32 = jnp.float32


def iota(shape, dim):
    return lax.broadcasted_iota(jnp.int32, shape, dim)


def shaped(rows, columns, dtype=BF16):
    return jax.ShapeDtypeStruct((rows, columns), dtype)


def call(kernel, outs, ins, after=(), scratch=(), room=6 * MIB, cost=None):
    count = len(ins)

    def body(*refs):
        kernel(*refs[:count], *refs[count + len(after):])

    integers = lambda a: a.ndim == 1 and a.dtype == jnp.int32
    specs = [pl.BlockSpec(memory_space=pltpu.SMEM if integers(a) else pltpu.VMEM) for a in ins]
    return pl.pallas_call(
        body,
        out_shape=outs,
        in_specs=specs + [pl.BlockSpec(memory_space=pl.ANY)] * len(after),
        out_specs=[pl.BlockSpec(memory_space=pltpu.VMEM)] * len(outs),
        scratch_shapes=list(scratch),
        compiler_params=pltpu.CompilerParams(vmem_limit_bytes=room),
        cost_estimate=cost,
    )(*ins, *after)


def part_of(ref, index, count):
    width = ref.shape[1] // count
    return ref[:, pl.ds(pl.multiple_of(index * width, width), width)]


def own_rows(rows, q_width, kv_width, block):
    return [0, rows, rows + block, rows + block + rows * q_width // kv_width, 16 + rows + block + rows * q_width // kv_width]


def pack_kernel(n_head, lengths, pages, k_ref, v_ref, q_ref, ck_ref, cv_ref, *outs):
    fresh, query, (cache, own) = outs[:n_head - 1], outs[n_head - 1:-2], outs[-2:]
    head = lax.axis_index("head")
    rows, (tokens, width) = k_ref.shape[0], ck_ref.shape
    kv_width, count = 2 * width, pages.shape[0]
    q_width = q_ref.shape[1] // n_head
    _, own_cache, own_query, own_ends, _ = own_rows(rows, q_width, kv_width, tokens + count)
    page = iota((count, kv_width), 0)
    owner = jnp.zeros((count, kv_width), jnp.int32)
    for p in range(count):
        owner = jnp.where(page == p, pages[p], owner)
    owner = owner.astype(F32).astype(BF16)
    for out, start in ((cache, 0), (own, own_cache)):
        out[start:start + tokens, :width] = ck_ref[...]
        out[start:start + tokens, width:] = cv_ref[...]
        out[start + tokens:start + tokens + count, :] = owner
    for x, out in enumerate([own, *fresh]):
        out[:rows, :width] = part_of(k_ref, head ^ x, n_head)
        out[:rows, width:] = part_of(v_ref, head ^ x, n_head)
    for x, out in enumerate(query, 1):
        out[...] = part_of(q_ref, head ^ x, n_head)
    mine = part_of(q_ref, head, n_head)
    for i in range(q_width // kv_width):
        own[own_query + i * rows:own_query + (i + 1) * rows, :] = mine[:, i * kv_width:(i + 1) * kv_width]
    row, low = iota((16, kv_width), 0), iota((16, kv_width), 1) >= LANES
    end, filled = 0, jnp.zeros((16, kv_width), jnp.int32)
    for r in range(lengths.shape[0]):
        end = end + lengths[r]
        filled = jnp.where(row == r, jnp.where(low, end & 127, end >> 7), filled)
    own[own_ends:, :] = filled.astype(F32).astype(BF16)


def stage_kernel(own, fresh, cache, ends, query):
    rows, q_width = query.shape
    block, kv_width = cache.shape
    _, own_cache, own_query, own_ends, _ = own_rows(rows, q_width, kv_width, block)
    fresh[...] = own[:rows, :]
    cache[...] = own[own_cache:own_query, :]
    for i in range(q_width // kv_width):
        query[:, i * kv_width:(i + 1) * kv_width] = own[own_query + i * rows:own_query + (i + 1) * rows, :]
    digits = own[own_ends:, :].astype(F32).astype(jnp.int32)
    ends[...] = (digits[:, :LANES] * 128 + digits[:, LANES:2 * LANES])[:ends.shape[0]]


def stack_kernel(*refs):
    out, rows = refs[-1], refs[0].shape[0]
    for i, ref in enumerate(refs[:-1]):
        out[i * rows:(i + 1) * rows, :] = ref[...]


def stack(parts, *after):
    rows, columns = parts[0].shape
    return call(stack_kernel, [shaped(len(parts) * rows, columns)], parts, after=after)[0]


class Layout:
    def __init__(self, ends, rows, q_width, kv_width, n_ctx, n_head):
        self.rows, self.n_ctx, self.n_head = rows, n_ctx, n_head
        self.groups = kv_width // (2 * HD)
        self.repeat = q_width // (self.groups * HD)
        self.half = n_head * rows // 2
        self.c, self.h = lax.axis_index("ctx"), lax.axis_index("head")
        self.ends = [ends[r:r + 1, :] for r in range(ends.shape[0])]
        self.lane = iota((rows, LANES), 1)
        self.row = iota((rows, LANES), 0)
        self.row_lane = self.lane - (LANES - rows)

    def start_of(self, rank, head):
        first = head * self.rows < self.half
        piece = jnp.where(first, rank, 2 * self.n_ctx - 1 - rank)
        return piece * self.half + lax.rem(head * self.rows, self.half)

    def step_of(self, b):
        if self.n_ctx != 8 or self.n_head != 4:
            return b
        near = jnp.where(lax.rem(self.c, 2) == 0, 2, 4)
        return [0, near, 1, 7 - near, 6 - near, 6, 1 + near, 7][b]

    def request(self, position):
        request = jnp.zeros(position.shape, jnp.int32)
        for end in self.ends:
            request += (position >= end).astype(jnp.int32)
        return request

    def query_rows(self, query, x):
        q = query[...]
        own = self.lane == self.request(self.start_of(self.c, self.h ^ x) + self.row)
        mask = jnp.where(own | (self.row_lane == self.row), 1.0, 0.0).astype(BF16)
        result = []
        for g in range(self.groups):
            heads = [
                jnp.concatenate([q[:, n * HD:(n + 1) * HD], mask], axis=1)
                for n in range(g * self.repeat, (g + 1) * self.repeat)
            ]
            result.append(jnp.concatenate(heads, axis=0))
        return result

    def fresh_mask(self, b, head):
        p0 = self.start_of(self.c, head)
        parts = []
        for x in [0, *range(self.n_head - 1, 0, -1)]:
            position = self.start_of(self.c ^ self.step_of(b), self.h ^ x) + self.row
            other = (self.lane < len(self.ends)) & (self.request(position) != self.lane)
            later = (self.row_lane >= 0) & (position > p0 + self.row_lane)
            parts.append(jnp.where(other | later, HIDDEN, 0.0))
        return jnp.concatenate(parts, axis=0).astype(BF16)

    def cache_mask(self, owner):
        pages = owner.shape[0]
        lane = iota((pages, LANES), 1)
        other = (lane < len(self.ends)) & (owner.astype(F32) != lane.astype(F32))
        bias = jnp.where(other, HIDDEN, 0.0)
        bias = jnp.broadcast_to(bias[:, None, :], (pages, PAGE, LANES))
        return bias.reshape(pages * PAGE, LANES).astype(BF16)


def attend(q_rows, blocks, masks, scores, tokens, g, groups):
    scale = math.log2(math.e) / math.sqrt(HD)
    largest = None
    for b, (block, mask) in enumerate(zip(blocks, masks)):
        keys = jnp.concatenate([block[:tokens, g * HD:(g + 1) * HD], mask[...]], axis=1)
        s = lax.dot_general(q_rows, keys, (((1,), (1,)), ((), ())), preferred_element_type=F32)
        scores[:, b * tokens:(b + 1) * tokens] = s
        for t in range(tokens // LANES):
            part = s[:, t * LANES:(t + 1) * LANES]
            largest = part if largest is None else jnp.maximum(largest, part)
    top = jnp.max(largest, axis=1, keepdims=True) * scale
    ones = jnp.ones((tokens, HD), BF16)
    summed = jnp.zeros((q_rows.shape[0], 2 * HD), F32)
    for b, block in enumerate(blocks):
        weights = jnp.exp2(scores[:, b * tokens:(b + 1) * tokens] * scale - top).astype(BF16)
        values = jnp.concatenate([block[:tokens, (groups + g) * HD:(groups + g + 1) * HD], ones], axis=1)
        summed += jnp.dot(weights, values, preferred_element_type=F32)
    return summed, jnp.broadcast_to(top, (q_rows.shape[0], LANES))


def views(refs, tokens):
    return [ref.at[pl.ds(i, tokens)] for ref in refs for i in range(0, ref.shape[0], tokens)]


def first_kernel(xs, cached, count, skip, n_ctx, n_head, q_width, ends, *refs):
    query, refs = refs[:len(xs)], refs[len(xs):]
    outs, (scores, masks) = refs[count:-2], refs[-2:]
    tokens = masks.shape[1]
    cache = views(refs[:cached], tokens + tokens // PAGE)
    fresh = views(refs[cached:count], tokens)
    at = Layout(ends, query[0].shape[0], q_width, refs[0].shape[1], n_ctx, n_head)
    blocks = cache + fresh
    for b in range(len(cache)):
        masks[b] = at.cache_mask(cache[b][tokens:, :LANES])
    for i, x in enumerate(xs):
        summed, tops = outs[2 * i:2 * i + 2]
        for b in range(len(fresh)):
            masks[len(cache) + b] = at.fresh_mask(skip + b, at.h ^ x)
        q_rows = at.query_rows(query[i], x)
        for g in range(at.groups):
            summed[g], tops[g] = attend(
                q_rows[g], blocks, [masks.at[b] for b in range(len(blocks))], scores.at[g], tokens, g, at.groups
            )


def last_kernel(xs, count, states, n_ctx, n_head, q_width, ends, *refs):
    query, refs = refs[:len(xs)], refs[len(xs):]
    split = count + 2 * states * len(xs)
    fresh, state, refs = refs[:count], refs[count:split], refs[split:]
    weight, outs, (scores, masks, mixed) = refs[0], refs[1:-3], refs[-3:]
    rows, tokens = query[0].shape[0], masks.shape[1]
    fresh = views(fresh, tokens)
    at = Layout(ends, rows, q_width, fresh[0].shape[1], n_ctx, n_head)
    for i, x in enumerate(xs):
        earlier = state[2 * states * i:2 * states * (i + 1)]
        for b in range(len(fresh)):
            masks[b] = at.fresh_mask(n_ctx - len(fresh) + b, at.h ^ x)
        q_rows = at.query_rows(query[i], x)
        for g in range(at.groups):
            sum_b, top_b = attend(
                q_rows[g], fresh, [masks.at[b] for b in range(len(fresh))], scores.at[g], tokens, g, at.groups
            )
            top = top_b
            for tops in earlier[1::2]:
                top = jnp.maximum(top, tops[g])
            joined = sum_b * jnp.concatenate([jnp.exp2(top_b - top)] * 2, axis=1)
            for summed, tops in zip(earlier[::2], earlier[1::2]):
                joined += summed[g] * jnp.concatenate([jnp.exp2(tops[g] - top)] * 2, axis=1)
            value, total = joined[:, :HD], joined[:, HD:]
            attended = (value / total).astype(BF16)
            for j in range(at.repeat):
                n = g * at.repeat + j
                mixed[i * rows:(i + 1) * rows, n * HD:(n + 1) * HD] = attended[j * rows:(j + 1) * rows]
    width = outs[0].shape[1]
    step = min(1024, width)
    for n in range(width // step):
        columns = slice(n * step, (n + 1) * step)
        y = jnp.dot(mixed[...], weight[:, columns], preferred_element_type=F32).astype(BF16)
        for i, out in enumerate(outs):
            out[:, columns] = y[i * rows:(i + 1) * rows]


def add_kernel(count, *refs):
    out, rest = refs[-1], refs[count:-1]
    total = refs[0][...].astype(F32)
    for ref in refs[1:count]:
        total += ref[...].astype(F32)
    out[...] = total.astype(BF16)
    for ref in rest:
        head = lax.axis_index("head")

        @pl.when((head == 0) | (head == lax.axis_size("head") - 1))
        def _():
            out[...] = (total + ref[...].astype(F32)).astype(BF16)


def add(parts, at_ends=()):
    return call(functools.partial(add_kernel, len(parts)), [shaped(*parts[0].shape)], [*parts, *at_ends])[0]


def swap(value, axis, mask):
    return lax.ppermute(value, axis, [(i, i ^ mask) for i in range(lax.axis_size(axis))])


def leg(block, first):
    odd, even = (4, 2) if first else (2, 4)
    return lax.ppermute(block, "ctx", [(i, i ^ (odd if i % 2 else even)) for i in range(8)])


def gather(block):
    n_ctx = lax.axis_size("ctx")
    blocks = [block if m == 0 else swap(block, "ctx", m) for m in range(0, n_ctx, 2)]
    return [b for pair in blocks for b in (pair, swap(pair, "ctx", 1))]


def finish_kernel(count, *refs):
    out, total, sems = refs[-3:]
    head = lax.axis_index("head")
    last = refs[count]
    step = out.shape[1] // 4
    copies = []
    for n in range(4):
        columns = pl.ds(n * step, step)
        part = refs[0][:, columns].astype(F32)
        for ref in refs[1:count]:
            part += ref[:, columns].astype(F32)
        at_end = (head == 0) | (head == lax.axis_size("head") - 1)
        part += jnp.where(at_end, last[:, columns].astype(F32), 0.0)
        total[:, columns] = part.astype(BF16)
        copies.append(pltpu.make_async_copy(total.at[:, columns], out.at[:, columns], sems.at[n]))
        copies[-1].start()
    for copy in copies:
        copy.wait()


def finish(parts, at_ends):
    shape = parts[0].shape
    return pl.pallas_call(
        functools.partial(finish_kernel, len(parts)),
        out_shape=shaped(*shape),
        in_specs=[pl.BlockSpec(memory_space=pltpu.VMEM)] * (len(parts) + 1),
        out_specs=pl.BlockSpec(memory_space=pl.ANY),
        scratch_shapes=[pltpu.VMEM(shape, BF16), pltpu.SemaphoreType.DMA((4,))],
        compiler_params=pltpu.CompilerParams(vmem_limit_bytes=6 * MIB),
    )(*parts, at_ends)


def send(value, pairs):
    return lax.ppermute(value, "head", pairs)


def scatter_line(part):
    next_inner, = part((2,))
    first = send(next_inner, [(0, 1), (1, 3), (2, 0), (3, 2)])
    far, = part((3,), next_inner)
    ends = send(far, [(0, 3), (3, 0)])
    near, = part((1,), far)
    own, = part((0,), near)
    near = send(near, [(0, 1), (1, 0), (2, 3), (3, 2)])
    middle = send(add([far, first]), [(1, 2), (2, 1)])
    return finish([own, near, ends, middle], first)


def scatter_direct(part, n_head):
    parts = []
    for x in [*range(n_head - 1, 0, -1), 0]:
        got, = part((x,))
        parts.append(swap(got, "head", x) if x else got)
    return add(parts)


def shards(queries, fresh_keys, fresh_values, cache_keys, cache_values, page_request, prompt_lengths, output_weight):
    n_ctx, n_head = lax.axis_size("ctx"), lax.axis_size("head")
    rows, columns = queries.shape[0], output_weight.shape[1]
    tokens, pages = cache_keys.shape[0], page_request.shape[0]
    kv_width = 2 * fresh_keys.shape[1] // n_head
    q_width = queries.shape[1] // n_head
    groups = kv_width // (2 * HD)
    stacked = q_width // (groups * HD) * rows
    keys = n_ctx * tokens

    own = shaped(own_rows(rows, q_width, kv_width, tokens + pages)[-1], kv_width)
    *packed, sent, own = call(
        functools.partial(pack_kernel, n_head),
        [shaped(rows, kv_width)] * (n_head - 1) + [shaped(rows, q_width)] * (n_head - 1) + [shaped(tokens + pages, kv_width), own],
        [prompt_lengths, page_request, fresh_keys, fresh_values, queries, cache_keys, cache_values], room=58 * MIB,
    )
    fresh, cache, ends, *query = call(
        stage_kernel,
        [shaped(rows, kv_width), shaped(tokens + pages, kv_width), shaped(prompt_lengths.shape[0], LANES, jnp.int32)]
        + [shaped(rows, q_width)],
        [own],
    )
    query += packed[n_head - 1:]

    fresh = stack([fresh, *(swap(packed[x - 1], "head", x) for x in range(n_head - 1, 0, -1))])
    for x in range(1, n_head):
        query[x] = swap(query[x], "head", x)
    square = n_ctx == 8 and n_head == 4
    if square:
        beside, across = leg(sent, True), leg(sent, False)
        corner = leg(stack([beside], fresh), False)
        got = leg(fresh, True)
        cache = stack([cache, beside, across, corner], got, *query[1:3])
        cache = [cache, swap(cache, "ctx", 1)]
        fresh = stack([fresh, got])
        early, late = [fresh, swap(fresh, "ctx", 1)], [leg(fresh, False)]
    else:
        cache, fresh = gather(sent), gather(fresh)
        early, late = fresh[:n_ctx // 2], fresh[n_ctx // 2:]

    attend_keys = lambda n: dict(
        scratch=[pltpu.VMEM((groups, stacked, n * tokens), F32), pltpu.VMEM((n, tokens, LANES), BF16)],
        room=4 * groups * stacked * n * tokens + 6 * MIB,
    )

    state = {}

    def first(xs, *after):
        n = n_ctx + n_ctx // 2
        found = call(
            functools.partial(first_kernel, xs, len(cache), len(cache) + len(early), 0, n_ctx, n_head, q_width),
            [jax.ShapeDtypeStruct((groups, stacked, lanes), F32) for _ in xs for lanes in (2 * HD, LANES)],
            [ends, *(query[x] for x in xs), *cache, *early], after=after, **attend_keys(n),
            cost=pl.CostEstimate(
                flops=16 * len(xs) * rows * q_width * n * tokens,
                bytes_accessed=2 * n * tokens * kv_width,
                transcendentals=len(xs) * rows * (q_width // HD) * n * tokens,
            ),
        )
        state.update((x, found[2 * i:2 * i + 2]) for i, x in enumerate(xs))

    def part(xs, *after):
        states = len(state[xs[0]]) // 2
        blocks = late[states - 1:]
        n = sum(block.shape[0] for block in blocks) // tokens
        options = attend_keys(n)
        options["scratch"].append(pltpu.VMEM((len(xs) * rows, q_width), BF16))
        return call(
            functools.partial(last_kernel, xs, len(blocks), states, n_ctx, n_head, q_width), [shaped(rows, columns)] * len(xs),
            [ends, *(query[x] for x in xs), *blocks, *(a for x in xs for a in state[x]), output_weight],
            after=after, **options,
            cost=pl.CostEstimate(
                flops=len(xs) * (16 * rows * q_width * n * tokens + 8 * rows * q_width * columns),
                bytes_accessed=2 * n * tokens * kv_width,
                transcendentals=len(xs) * rows * (q_width // HD) * n * tokens,
            ),
        )

    if square:
        first((2,))
        late = [stack(late, state[2][1], query[3])]
        late.append(swap(late[0], "ctx", 1))
        n = late[0].shape[0] // tokens
        state[2] = state[2] + call(
            functools.partial(first_kernel, (2,), 0, 1, n_ctx - 2 * n, n_ctx, n_head, q_width),
            [jax.ShapeDtypeStruct((groups, stacked, lanes), F32) for lanes in (2 * HD, LANES)],
            [ends, query[2], late[0]], **attend_keys(n),
        )

    def chunks(xs, *after):
        todo = tuple(x for x in xs if x not in state)
        if todo:
            first(todo, *after)
        return part(xs, *after)

    return scatter_line(chunks) if square else scatter_direct(chunks, n_head)


def solution(mesh):
    placed = (
        P(("ctx", "head"), None),
        P(("ctx", "head"), None),
        P(("ctx", "head"), None),
        P("ctx", "head"),
        P("ctx", "head"),
        P("ctx"),
        P(),
        P("head", None),
    )
    return jax.shard_map(
        shards, mesh=mesh, in_specs=placed, out_specs=P(("ctx", "head"), None), check_vma=False
    )
```
